128 devices in a mesh: row: 8 (over z, core), col: 16 (over y, x).
Axes of the slice: x: 4, y: 4, z: 4, core: 2. Of those that a mesh axis runs over, the one named last changes fastest.
Arguments:
- slab: float32 [16384, 8192], P(('row', 'col')), may hold values from -6 to 6
- block_mask: int32 [128, 64], P(('row', 'col')), may hold values 0 or 1
Outputs:
- band_gram: float32 [2048, 8192], P('row', 'col')
- factor: float32 [2048, 2048], P('row', 'col')
The draws below stay inside these ranges and needn't reach their ends.
All inputs are finite; a program needn't handle non-finite values. No bound on the sum of `block_mask` on one device may be relied on, other than what follows from the above.
Results may differ from the reference program's by a relative error of at most 0.000073.
Values sent between devices are 32-bit elements; how exact they have to be, the bound alone decides.
No kernel may reach another device: no remote copies, remote signals or barrier semaphores. Data moves between devices by JAX's collectives and lax.ppermute only.
A program may use at most 192 MiB of HBM per device.

```python
import jax
import jax.numpy as jnp
from jax import lax

BLK = 128
U_DEV = 128
IC = 512
SHIFT_NUM = 2
USERS = 16384
ITEMS = 8192
BAND = 2048
N_COL = 16
DEVICES = 128


def plant(drawn, own_key, low, high):
    shape = drawn.shape
    place = [jax.random.randint(jax.random.fold_in(own_key, axis), (), 0, shape[axis]) for axis in range(len(shape))]
    drawn = drawn.at[tuple(place)].set(low)
    longest = shape.index(max(shape))
    place[longest] = (place[longest] + 1) % shape[longest]
    return drawn.at[tuple(place)].set(high)


def block_levels(own_key, shape, pieces, least, largest):
    level, own = 1.0, jax.random.fold_in(own_key, 6)
    for dim, shards_of in pieces:
        draws = jnp.exp(jax.random.uniform(jax.random.fold_in(own, dim), (shards_of,), jnp.float32, least / len(pieces), largest / len(pieces)))
        level = level * jnp.repeat(draws, shape[dim] // shards_of).reshape([-1 if axis == dim else 1 for axis in range(len(shape))])
    return level


def gaussian(own_key, extent, width, reach, split=(), kind=jnp.bfloat16):
    factor_of = block_levels(own_key, extent, split, -0.22, 0.18) if split else 1.0
    array = jax.random.normal(own_key, extent, jnp.float32) * width * factor_of
    return jnp.minimum(jnp.maximum(array, -reach), reach).astype(kind)


def setup_inputs(seed: int = 0) -> dict:
    arg_keys = jax.random.split(jax.random.key(seed), 3)
    slab = gaussian(arg_keys[0], (USERS, ITEMS), 1.0, 6.0, ((0, 128),), jnp.float32)
    block_mask = plant((jax.random.randint(arg_keys[1], (DEVICES, ITEMS // BLK), 0, 4) < 3).astype(jnp.int32), jax.random.fold_in(arg_keys[1], 1), 0, 1)
    return dict(slab=slab, block_mask=block_mask)


def reference(slab, block_mask):
    keep = jnp.repeat(block_mask.astype(jnp.float32), BLK, axis=1)
    keep = jnp.repeat(keep, U_DEV, axis=0)
    dense = slab * keep
    band = (jnp.arange(N_COL, dtype=jnp.int32)[:, None] * IC + jnp.arange(BLK, dtype=jnp.int32)[None, :]).reshape(-1)
    band_cols = dense[:, band]
    band_gram = jnp.dot(band_cols.T.astype(jnp.float32), dense.astype(jnp.float32), precision=lax.Precision.HIGHEST, preferred_element_type=jnp.float32) / USERS
    panel = band_gram[:, band] + SHIFT_NUM / 4.0 * jnp.eye(BAND, dtype=jnp.float32)
    factor = jnp.linalg.cholesky(panel)
    return (band_gram, factor)
```

```python
import functools

import jax
import jax.numpy as jnp
from jax import lax
from jax.experimental import pallas as pl
from jax.experimental.pallas import tpu as pltpu
from jax.sharding import PartitionSpec as P

BLK = 128
SHIFT_NUM = 2

def diag128(F):
    S = (8, 128)
    lane = lax.broadcasted_iota(jnp.int32, S, 1)
    subl = lax.broadcasted_iota(jnp.int32, S, 0)
    F = list(F)
    Ws = []
    onehot = [jnp.where(subl == k, 1.0, 0.0) for k in range(8)]
    n = len(F)
    for t in range(n):
        b = 8 * t
        C = {s: [jnp.broadcast_to(F[s][:, b + k:b + k + 1], S) for k in range(8)] for s in range(t, n)}
        inblk = (lane >= b) & (lane < b + 8)
        X = jnp.where(inblk, jnp.where(lane - b == subl, 1.0, 0.0), F[t])
        D = C[t]
        G = jnp.zeros(S, jnp.float32)
        for k in range(8):
            d = jnp.broadcast_to(D[k][k:k + 1], S)
            rs = lax.rsqrt(d)
            inv = rs * rs
            g = D[k] - onehot[k]
            xk = jnp.broadcast_to(X[k:k + 1], S)
            G = jnp.where(subl == k, xk * rs, G)
            X = X - g * (xk * inv)
            for m in range(k + 1, 8):
                r = jnp.broadcast_to(D[m][k:k + 1], S)
                D[m] = D[m] - g * (r * inv)
        Ws.append(jnp.where(lane < b + 8, G, 0.0))
        V = [jnp.broadcast_to(X[k:k + 1], S) for k in range(8)]
        for s in range(t + 1, n):
            f = jnp.where(inblk, 0.0, F[s])
            for k in range(8):
                f = f - C[s][k] * V[k]
            F[s] = f
    return Ws

def split(x, n):
    parts = []
    for i in range(n):
        h = x.astype(jnp.bfloat16)
        parts.append(h)
        if i + 1 < n:
            x = x - h.astype(jnp.float32)
    return parts

PAIRS = {2: [(0, 0), (0, 1), (1, 0)], 3: [(0, 0), (0, 1), (1, 0), (0, 2), (1, 1), (2, 0)]}

def dot_nt(a, b):
    pairs = PAIRS[len(a)]
    x = jnp.concatenate([a[i] for i, _ in pairs], axis=1)
    y = jnp.concatenate([b[j] for _, j in pairs], axis=1)
    return lax.dot_general(x, y, (((1,), (1,)), ((), ())), preferred_element_type=jnp.float32)

BT = 512

def chol_kernel(nparts, place_ref, a_ref, out_ref, *scratch):
    Ls = scratch[:nparts]
    P, W = scratch[nparts:]
    n = a_ref.shape[0]
    r = place_ref[0]
    c = place_ref[1]

    def zero(i, _):
        for L in Ls:
            L[pl.ds(i * 128, 128), :] = jnp.zeros((128, n), L.dtype)
        return 0
    lax.fori_loop(0, n // 128, zero, 0)
    out_ref[...] = jnp.zeros(out_ref.shape, jnp.float32)

    def column(jj, _):
        J2 = jj // 2
        h = jj % 2
        base = pl.multiple_of(J2 * 256, 256)
        here = pl.multiple_of(jj * 128, 128)
        first = base // BT

        @pl.when(h == 0)
        def _():
            def rows(i, _):
                at = pl.ds(pl.multiple_of(i * BT, BT), BT)
                P[at, :] = a_ref[at, pl.ds(base, 256)]
                def depth(q, _):
                    ks = pl.ds(pl.multiple_of(q * 512, 512), 512)
                    P[at, :] -= dot_nt([L[at, ks] for L in Ls], [L[pl.ds(base, 256), ks] for L in Ls])
                    return 0
                lax.fori_loop(0, (base + 511) // 512, depth, 0)
                return 0
            lax.fori_loop(first, n // BT, rows, 0)

        @pl.when(h == 1)
        def _():
            prev = pl.ds(pl.multiple_of(here - 128, 128), 128)
            def rows(i, _):
                at = pl.ds(pl.multiple_of(i * BT, BT), BT)
                P[at, 128:] -= dot_nt([L[at, prev] for L in Ls], [L[pl.ds(here, 128), prev] for L in Ls])
                return 0
            lax.fori_loop(first, n // BT, rows, 0)
            P[:, :128] = P[:, 128:]

        ws = diag128([P[pl.ds(pl.multiple_of(here + 8 * s, 8), 8), :128] for s in range(16)])
        for s in range(16):
            W[8 * s:8 * s + 8, :] = ws[s]
        w = split(W[...], 3)

        def rows(i, _):
            at = pl.ds(pl.multiple_of(i * BT, BT), BT)
            l = dot_nt(split(P[at, :128], 3), w)
            for L, part in zip(Ls, split(l, nparts)):
                L[at, pl.ds(here, 128)] = part
            P[at, :128] = l
            return 0
        lax.fori_loop(first, n // BT, rows, 0)

        @pl.when(jj == c)
        def _():
            rows = out_ref.shape[0]
            mine = P[pl.ds(pl.multiple_of(r * rows, rows), rows), :128]
            row = lax.broadcasted_iota(jnp.int32, mine.shape, 0) + r * rows
            col = lax.broadcasted_iota(jnp.int32, mine.shape, 1) + here
            out_ref[...] = jnp.where(row >= col, mine, 0.0)
        return 0
    lax.fori_loop(0, n // 128, column, 0)

def chol_piece(panel, place, rows, nparts=3):
    n = panel.shape[0]
    return pl.pallas_call(
        functools.partial(chol_kernel, nparts),
        out_shape=jax.ShapeDtypeStruct((rows, 128), jnp.float32),
        in_specs=[pl.BlockSpec(memory_space=pltpu.SMEM), pl.BlockSpec(memory_space=pltpu.VMEM)],
        out_specs=pl.BlockSpec(memory_space=pltpu.VMEM),
        scratch_shapes=[pltpu.VMEM((n, n), jnp.bfloat16)] * nparts + [pltpu.VMEM((n, 256), jnp.float32), pltpu.VMEM((128, 128), jnp.float32)],
        compiler_params=pltpu.CompilerParams(vmem_limit_bytes=56 * 2**20),
        name="factor",
    )(place, panel)


def shards(slab, block_mask):
    items = slab.shape[1]
    blocks = block_mask.shape[1]
    width = items // blocks
    keep = jnp.broadcast_to(block_mask.astype(jnp.float32)[:, :, None], (1, blocks, width)).reshape(
        1, items
    )
    dense = slab * keep
    ncols = lax.axis_size("col")
    nrows = lax.axis_size("row")
    local = lax.all_to_all(dense, "col", split_axis=1, concat_axis=0, tiled=True)
    band_cols = lax.all_gather(local[:, :BLK], "col", axis=1, tiled=True)
    partial_gram = jnp.dot(
        band_cols.T, local, precision=lax.Precision.HIGHEST, preferred_element_type=jnp.float32
    )
    total_users = local.shape[0] * nrows
    tile = lax.psum_scatter(partial_gram, "row", scatter_dimension=0, tiled=True) / total_users
    band_width = BLK * ncols
    strip = lax.all_gather(tile[:, :BLK], "col", axis=1, tiled=True)
    panel = lax.all_gather(strip, "row", axis=0, tiled=True)
    panel = panel + SHIFT_NUM / 4.0 * jnp.eye(band_width, dtype=jnp.float32)
    row_count = band_width // nrows
    place = jnp.stack([lax.axis_index("row"), lax.axis_index("col")]).astype(jnp.int32)
    piece = chol_piece(panel, place, row_count)
    return (tile, piece)


def solution(mesh):
    placed = (P(("row", "col"), None), P(("row", "col"), None))
    return jax.shard_map(
        shards,
        mesh=mesh,
        in_specs=placed,
        out_specs=(P("row", "col"), P("row", "col")),
        check_vma=False,
    )
```

```python
import functools

import jax
import jax.numpy as jnp
from jax import lax
from jax.experimental import pallas as pl
from jax.experimental.pallas import tpu as pltpu
from jax.sharding import PartitionSpec as P

BLK = 128
SHIFT_NUM = 2


def diag128(F):
    S = (8, 128)
    lane = lax.broadcasted_iota(jnp.int32, S, 1)
    subl = lax.broadcasted_iota(jnp.int32, S, 0)
    F = list(F)
    Ws = []
    onehot = [jnp.where(subl == k, 1.0, 0.0) for k in range(8)]
    n = len(F)
    for t in range(n):
        b = 8 * t
        C = {s: [jnp.broadcast_to(F[s][:, b + k:b + k + 1], S) for k in range(8)] for s in range(t, n)}
        inblk = (lane >= b) & (lane < b + 8)
        X = jnp.where(inblk, jnp.where(lane - b == subl, 1.0, 0.0), F[t])
        D = C[t]
        G = jnp.zeros(S, jnp.float32)
        for k in range(8):
            d = jnp.broadcast_to(D[k][k:k + 1], S)
            rs = lax.rsqrt(d)
            inv = rs * rs
            g = D[k] - onehot[k]
            xk = jnp.broadcast_to(X[k:k + 1], S)
            G = jnp.where(subl == k, xk * rs, G)
            X = X - g * (xk * inv)
            for m in range(k + 1, 8):
                r = jnp.broadcast_to(D[m][k:k + 1], S)
                D[m] = D[m] - g * (r * inv)
        Ws.append(jnp.where(lane < b + 8, G, 0.0))
        V = [jnp.broadcast_to(X[k:k + 1], S) for k in range(8)]
        for s in range(t + 1, n):
            f = jnp.where(inblk, 0.0, F[s])
            for k in range(8):
                f = f - C[s][k] * V[k]
            F[s] = f
    return Ws

def split(x, n):
    parts = []
    for i in range(n):
        h = x.astype(jnp.bfloat16)
        parts.append(h)
        if i + 1 < n:
            x = x - h.astype(jnp.float32)
    return parts

PAIRS = {2: [(0, 0), (0, 1), (1, 0)], 3: [(0, 0), (0, 1), (1, 0), (0, 2), (1, 1), (2, 0)]}

def dot_nt(a, b):
    pairs = PAIRS[len(a)]
    x = jnp.concatenate([a[i] for i, _ in pairs], axis=1)
    y = jnp.concatenate([b[j] for _, j in pairs], axis=1)
    return lax.dot_general(x, y, (((1,), (1,)), ((), ())), preferred_element_type=jnp.float32)

BT = 512


def chol_kernel(nparts, place_ref, packed_ref, band_ref, out_ref, a_ref, *scratch):
    Ls = scratch[:nparts]
    P, W, sems = scratch[nparts:]
    n = a_ref.shape[0]
    nb = n // BLK
    r = place_ref[0]
    c = place_ref[1]

    copies = []
    for i in range(nb):
        src = min(i, nb - 1 - i)
        first = 0 if 2 * i >= nb else BLK * (nb - i)
        copies.append(
            pltpu.make_async_copy(
                packed_ref.at[pl.ds(BLK * src, BLK), pl.ds(first, BLK * (i + 1))],
                a_ref.at[pl.ds(BLK * i, BLK), pl.ds(0, BLK * (i + 1))],
                sems.at[i],
            )
        )
    for copy in copies:
        copy.start()

    def zero(i, _):
        for L in Ls:
            L[pl.ds(i * 128, 128), :] = jnp.zeros((128, n), L.dtype)
        return 0

    lax.fori_loop(0, nb, zero, 0)
    out_ref[...] = jnp.zeros(out_ref.shape, jnp.float32)
    for copy in copies:
        copy.wait()

    for q in range(2):
        i = 2 * r + q
        rows_i = pl.multiple_of(i * BLK, BLK)
        cols_c = pl.multiple_of(c * BLK, BLK)

        @pl.when(c <= i)
        def _():
            band_ref[q * BLK:(q + 1) * BLK, :] = a_ref[pl.ds(rows_i, BLK), pl.ds(cols_c, BLK)]

        @pl.when(c > i)
        def _():
            band_ref[q * BLK:(q + 1) * BLK, :] = a_ref[pl.ds(cols_c, BLK), pl.ds(rows_i, BLK)].T

    row_of = lax.broadcasted_iota(jnp.int32, (BLK, BLK), 0)
    col_of = lax.broadcasted_iota(jnp.int32, (BLK, BLK), 1)
    shift = jnp.where(row_of == col_of, SHIFT_NUM / 4.0, 0.0)

    def column(jj, _):
        J2 = jj // 2
        h = jj % 2
        base = pl.multiple_of(J2 * 256, 256)
        here = pl.multiple_of(jj * 128, 128)
        first = base // BT

        @pl.when(h == 0)
        def _():
            def rows(i, _):
                at = pl.ds(pl.multiple_of(i * BT, BT), BT)
                P[at, :] = a_ref[at, pl.ds(base, 256)]

                def depth(q, _):
                    ks = pl.ds(pl.multiple_of(q * 512, 512), 512)
                    P[at, :] -= dot_nt([L[at, ks] for L in Ls], [L[pl.ds(base, 256), ks] for L in Ls])
                    return 0

                lax.fori_loop(0, (base + 511) // 512, depth, 0)
                return 0

            lax.fori_loop(first, n // BT, rows, 0)

        @pl.when(h == 1)
        def _():
            prev = pl.ds(pl.multiple_of(here - 128, 128), 128)

            def rows(i, _):
                at = pl.ds(pl.multiple_of(i * BT, BT), BT)
                P[at, :128] = P[at, 128:] - dot_nt([L[at, prev] for L in Ls], [L[pl.ds(here, 128), prev] for L in Ls])
                return 0

            lax.fori_loop(first, n // BT, rows, 0)

        P[pl.ds(here, BLK), :BLK] += shift
        ws = diag128([P[pl.ds(pl.multiple_of(here + 8 * s, 8), 8), :128] for s in range(16)])
        for s in range(16):
            W[8 * s:8 * s + 8, :] = ws[s]
        w = split(W[...], 3)

        def rows(i, _):
            at = pl.ds(pl.multiple_of(i * BT, BT), BT)
            l = dot_nt(split(P[at, :128], 3), w)
            for L, part in zip(Ls, split(l, nparts)):
                L[at, pl.ds(here, 128)] = part
            P[at, :128] = l
            return 0

        lax.fori_loop(first, n // BT, rows, 0)

        @pl.when(jj == c)
        def _():
            rows = out_ref.shape[0]
            mine = P[pl.ds(pl.multiple_of(r * rows, rows), rows), :128]
            row = lax.broadcasted_iota(jnp.int32, mine.shape, 0) + r * rows
            col = lax.broadcasted_iota(jnp.int32, mine.shape, 1) + here
            out_ref[...] = jnp.where(row >= col, mine, 0.0)

        return 0

    lax.fori_loop(0, nb, column, 0)


def chol_piece(packed, place, n, rows, nparts=3):
    nb = n // BLK
    flat = jax.ShapeDtypeStruct((rows, BLK), jnp.float32)
    vmem = pl.BlockSpec(memory_space=pltpu.VMEM)
    return pl.pallas_call(
        functools.partial(chol_kernel, nparts),
        out_shape=(flat, flat),
        in_specs=[pl.BlockSpec(memory_space=pltpu.SMEM), pl.BlockSpec(memory_space=pl.ANY)],
        out_specs=(vmem, vmem),
        scratch_shapes=[pltpu.VMEM((n, n), jnp.float32)]
        + [pltpu.VMEM((n, n), jnp.bfloat16)] * nparts
        + [pltpu.VMEM((n, 256), jnp.float32), pltpu.VMEM((BLK, BLK), jnp.float32), pltpu.SemaphoreType.DMA((nb,))],
        compiler_params=pltpu.CompilerParams(vmem_limit_bytes=56 * 2**20),
        cost_estimate=pl.CostEstimate(flops=2 * n * n * n, bytes_accessed=300 * 2**20, transcendentals=n),
        name="factor",
    )(place, packed)


def mask_kernel(keep_ref, slab_ref, band_ref, rest_ref):
    c = pl.program_id(0)
    per = slab_ref.shape[1] // BLK
    for b in range(per):
        part = slab_ref[:, b * BLK:(b + 1) * BLK] * keep_ref[0, c * per + b].astype(jnp.float32)
        if b == 0:
            band_ref[...] = part
        else:
            rest_ref[0, :, (b - 1) * BLK:b * BLK] = part


def mask_and_sort(slab, block_mask, ncols, nrows):
    users, items = slab.shape
    width = items // ncols
    other = width - BLK
    pair = ncols // nrows
    return pl.pallas_call(
        mask_kernel,
        grid=(ncols,),
        out_shape=(
            jax.ShapeDtypeStruct((users, BLK * ncols), jnp.float32),
            jax.ShapeDtypeStruct((nrows, users, pair * other), jnp.float32),
        ),
        in_specs=[pl.BlockSpec(memory_space=pltpu.SMEM), pl.BlockSpec((users, width), lambda c: (0, c))],
        out_specs=(
            pl.BlockSpec((users, BLK), lambda c: (0, c)),
            pl.BlockSpec((1, users, other), lambda c: (c // pair, 0, c % pair)),
        ),
        name="mask",
    )(block_mask, slab)


def shards(slab, block_mask):
    ncols = lax.axis_size("col")
    nrows = lax.axis_size("row")
    r = lax.axis_index("row")
    c = lax.axis_index("col")
    pair = ncols // nrows
    total_users = slab.shape[0] * ncols * nrows
    high = dict(precision=lax.Precision.HIGH, preferred_element_type=jnp.float32)
    over_users = (((0,), (0,)), ((), ()))

    band, rest = mask_and_sort(slab, block_mask, ncols, nrows)
    bands = lax.all_gather(band, "row", axis=0, tiled=True)

    upper = lax.dynamic_slice_in_dim(bands, BLK * r, BLK, 1)
    lower = lax.dynamic_slice_in_dim(bands, BLK * (ncols - 1 - r), BLK, 1)
    both = lax.dot_general(jnp.concatenate([lower, upper], axis=1), bands, over_users, **high)
    padded = jnp.concatenate([jnp.zeros((BLK, BLK * ncols), jnp.float32), both[BLK:]], axis=1)
    moved = lax.dynamic_slice_in_dim(padded, BLK * r, BLK * (ncols + 1), 1)
    long = jnp.concatenate([both[:BLK], jnp.zeros((BLK, BLK), jnp.float32)], axis=1)
    lane = lax.broadcasted_iota(jnp.int32, moved.shape, 1)
    packed = jnp.where(lane < BLK * (ncols - r), long, moved)
    pieces = lax.all_to_all(packed, "col", split_axis=0, concat_axis=0, tiled=True)
    mine = jnp.sum(pieces.reshape(ncols, BLK // ncols, -1), axis=0) / total_users
    mine, rest = lax.optimization_barrier((mine, rest))
    panel = lax.all_gather(mine, ("row", "col"), axis=0, tiled=True)

    others = lax.all_to_all(rest, "row", split_axis=0, concat_axis=0, tiled=True)
    others = others.reshape(-1, others.shape[-1])
    partial = lax.dot_general(bands, others, over_users, **high)
    strip = lax.psum_scatter(partial, "col", scatter_dimension=0, tiled=True) / total_users
    half = strip.shape[1] // pair
    odd = c % 2
    own = lax.dynamic_slice_in_dim(strip, half * odd, half, 1)
    far = lax.dynamic_slice_in_dim(strip, half * (1 - odd), half, 1)
    at = [(i, j) for i in range(nrows) for j in range(ncols)]
    to = lambda i, j: i * ncols + j
    own = lax.ppermute(own, ("row", "col"), [(to(i, j), to(j // 2, 2 * i + j % 2)) for i, j in at])
    far = lax.ppermute(far, ("row", "col"), [(to(i, j), to(j // 2, 2 * i + 1 - j % 2)) for i, j in at])
    items = jnp.where(odd == 0, jnp.concatenate([own, far]), jnp.concatenate([far, own]))

    place = jnp.stack([r, c]).astype(jnp.int32)
    block, piece = chol_piece(panel, place, BLK * ncols, BLK * pair)
    return (jnp.concatenate([block, items], axis=1), piece)


def solution(mesh):
    placed = (P(("row", "col"), None), P(("row", "col"), None))
    return jax.shard_map(
        shards,
        mesh=mesh,
        in_specs=placed,
        out_specs=(P("row", "col"), P("row", "col")),
        check_vma=False,
    )
```

```python
import functools

import jax
import jax.numpy as jnp
from jax import lax
from jax.experimental import pallas as pl
from jax.experimental.pallas import tpu as pltpu
from jax.sharding import PartitionSpec as P

BLK = 128
SHIFT_NUM = 2


def diag128(F):
    S = (8, 128)
    lane = lax.broadcasted_iota(jnp.int32, S, 1)
    subl = lax.broadcasted_iota(jnp.int32, S, 0)
    F = list(F)
    Ws = []
    onehot = [jnp.where(subl == k, 1.0, 0.0) for k in range(8)]
    n = len(F)
    for t in range(n):
        b = 8 * t
        C = {s: [jnp.broadcast_to(F[s][:, b + k:b + k + 1], S) for k in range(8)] for s in range(t, n)}
        inblk = (lane >= b) & (lane < b + 8)
        X = jnp.where(inblk, jnp.where(lane - b == subl, 1.0, 0.0), F[t])
        D = C[t]
        G = jnp.zeros(S, jnp.float32)
        for k in range(8):
            d = jnp.broadcast_to(D[k][k:k + 1], S)
            rs = lax.rsqrt(d)
            inv = rs * rs
            g = D[k] - onehot[k]
            xk = jnp.broadcast_to(X[k:k + 1], S)
            G = jnp.where(subl == k, xk * rs, G)
            X = X - g * (xk * inv)
            for m in range(k + 1, 8):
                r = jnp.broadcast_to(D[m][k:k + 1], S)
                D[m] = D[m] - g * (r * inv)
        Ws.append(jnp.where(lane < b + 8, G, 0.0))
        V = [jnp.broadcast_to(X[k:k + 1], S) for k in range(8)]
        for s in range(t + 1, n):
            f = jnp.where(inblk, 0.0, F[s])
            for k in range(8):
                f = f - C[s][k] * V[k]
            F[s] = f
    return Ws

def split(x, n):
    parts = []
    for i in range(n):
        h = x.astype(jnp.bfloat16)
        parts.append(h)
        if i + 1 < n:
            x = x - h.astype(jnp.float32)
    return parts

PAIRS = {2: [(0, 0), (0, 1), (1, 0)], 3: [(0, 0), (0, 1), (1, 0), (0, 2), (1, 1), (2, 0)]}

def dot_nt(a, b):
    pairs = PAIRS[len(a)]
    x = jnp.concatenate([a[i] for i, _ in pairs], axis=1)
    y = jnp.concatenate([b[j] for _, j in pairs], axis=1)
    return lax.dot_general(x, y, (((1,), (1,)), ((), ())), preferred_element_type=jnp.float32)

BT = 512


def chol_kernel(nparts, place_ref, packed_ref, band_ref, out_ref, a_ref, *scratch):
    Ls = scratch[:nparts]
    P, W, sems = scratch[nparts:]
    n = a_ref.shape[0]
    nb = n // BLK
    r = place_ref[0]
    c = place_ref[1]

    copies = []
    for i in range(nb):
        src = min(i, nb - 1 - i)
        first = 0 if 2 * i >= nb else BLK * (nb - i)
        copies.append(
            pltpu.make_async_copy(
                packed_ref.at[pl.ds(BLK * src, BLK), pl.ds(first, BLK * (i + 1))],
                a_ref.at[pl.ds(BLK * i, BLK), pl.ds(0, BLK * (i + 1))],
                sems.at[i],
            )
        )
    for copy in copies:
        copy.start()

    def zero(i, _):
        for L in Ls:
            L[pl.ds(i * 128, 128), :] = jnp.zeros((128, n), L.dtype)
        return 0

    lax.fori_loop(0, nb, zero, 0)
    out_ref[...] = jnp.zeros(out_ref.shape, jnp.float32)
    for copy in copies:
        copy.wait()

    for q in range(2):
        i = 2 * r + q
        rows_i = pl.multiple_of(i * BLK, BLK)
        cols_c = pl.multiple_of(c * BLK, BLK)

        @pl.when(c <= i)
        def _():
            band_ref[q * BLK:(q + 1) * BLK, :] = a_ref[pl.ds(rows_i, BLK), pl.ds(cols_c, BLK)]

        @pl.when(c > i)
        def _():
            band_ref[q * BLK:(q + 1) * BLK, :] = a_ref[pl.ds(cols_c, BLK), pl.ds(rows_i, BLK)].T

    row_of = lax.broadcasted_iota(jnp.int32, (BLK, BLK), 0)
    col_of = lax.broadcasted_iota(jnp.int32, (BLK, BLK), 1)
    shift = jnp.where(row_of == col_of, SHIFT_NUM / 4.0, 0.0)

    def column(jj, _):
        J2 = jj // 2
        h = jj % 2
        base = pl.multiple_of(J2 * 256, 256)
        here = pl.multiple_of(jj * 128, 128)
        first = base // BT

        @pl.when(h == 0)
        def _():
            def rows(i, _):
                at = pl.ds(pl.multiple_of(i * BT, BT), BT)
                P[at, :] = a_ref[at, pl.ds(base, 256)]

                def depth(q, _):
                    ks = pl.ds(pl.multiple_of(q * 512, 512), 512)
                    P[at, :] -= dot_nt([L[at, ks] for L in Ls], [L[pl.ds(base, 256), ks] for L in Ls])
                    return 0

                lax.fori_loop(0, (base + 511) // 512, depth, 0)
                return 0

            lax.fori_loop(first, n // BT, rows, 0)

        @pl.when(h == 1)
        def _():
            prev = pl.ds(pl.multiple_of(here - 128, 128), 128)

            def rows(i, _):
                at = pl.ds(pl.multiple_of(i * BT, BT), BT)
                P[at, :128] = P[at, 128:] - dot_nt([L[at, prev] for L in Ls], [L[pl.ds(here, 128), prev] for L in Ls])
                return 0

            lax.fori_loop(first, n // BT, rows, 0)

        P[pl.ds(here, BLK), :BLK] += shift
        ws = diag128([P[pl.ds(pl.multiple_of(here + 8 * s, 8), 8), :128] for s in range(16)])
        for s in range(16):
            W[8 * s:8 * s + 8, :] = ws[s]
        w = split(W[...], 3)

        def rows(i, _):
            at = pl.ds(pl.multiple_of(i * BT, BT), BT)
            l = dot_nt(split(P[at, :128], 3), w)
            for L, part in zip(Ls, split(l, nparts)):
                L[at, pl.ds(here, 128)] = part
            P[at, :128] = l
            return 0

        lax.fori_loop(first, n // BT, rows, 0)

        @pl.when(jj == c)
        def _():
            rows = out_ref.shape[0]
            mine = P[pl.ds(pl.multiple_of(r * rows, rows), rows), :128]
            row = lax.broadcasted_iota(jnp.int32, mine.shape, 0) + r * rows
            col = lax.broadcasted_iota(jnp.int32, mine.shape, 1) + here
            out_ref[...] = jnp.where(row >= col, mine, 0.0)

        return 0

    lax.fori_loop(0, nb, column, 0)


def chol_piece(packed, place, n, rows, nparts=3):
    nb = n // BLK
    flat = jax.ShapeDtypeStruct((rows, BLK), jnp.float32)
    vmem = pl.BlockSpec(memory_space=pltpu.VMEM)
    return pl.pallas_call(
        functools.partial(chol_kernel, nparts),
        out_shape=(flat, flat),
        in_specs=[pl.BlockSpec(memory_space=pltpu.SMEM), pl.BlockSpec(memory_space=pl.ANY)],
        out_specs=(vmem, vmem),
        scratch_shapes=[pltpu.VMEM((n, n), jnp.float32)]
        + [pltpu.VMEM((n, n), jnp.bfloat16)] * nparts
        + [pltpu.VMEM((n, 256), jnp.float32), pltpu.VMEM((BLK, BLK), jnp.float32), pltpu.SemaphoreType.DMA((nb,))],
        compiler_params=pltpu.CompilerParams(vmem_limit_bytes=56 * 2**20),
        cost_estimate=pl.CostEstimate(flops=2 * n * n * n, bytes_accessed=300 * 2**20, transcendentals=n),
        name="factor",
    )(place, packed)


def band_kernel(keep_ref, slab_ref, band_ref):
    band_ref[...] = slab_ref[...] * keep_ref[0, pl.program_id(0) * keep_ref.shape[1] // pl.num_programs(0)].astype(jnp.float32)


def band_columns(slab, block_mask, ncols):
    users, items = slab.shape
    step = items // ncols // BLK
    return pl.pallas_call(
        band_kernel,
        grid=(ncols,),
        out_shape=jax.ShapeDtypeStruct((users, BLK * ncols), jnp.float32),
        in_specs=[pl.BlockSpec(memory_space=pltpu.SMEM), pl.BlockSpec((users, BLK), lambda c: (0, c * step))],
        out_specs=pl.BlockSpec((users, BLK), lambda c: (0, c)),
        name="mask_band",
    )(block_mask, slab)


def rest_kernel(pair, keep_ref, slab_ref, rest_ref):
    g = pl.program_id(0)
    blocks = slab_ref.shape[1] // BLK
    per = blocks // pair
    to = 0
    for b in range(blocks):
        if b % per:
            keep = keep_ref[0, g * blocks + b].astype(jnp.float32)
            rest_ref[0, :, to:to + BLK] = slab_ref[:, b * BLK:(b + 1) * BLK] * keep
            to += BLK


def other_columns(slab, block_mask, ncols, nrows):
    users, items = slab.shape
    pair = ncols // nrows
    other = items // nrows - pair * BLK
    return pl.pallas_call(
        functools.partial(rest_kernel, pair),
        grid=(nrows,),
        out_shape=jax.ShapeDtypeStruct((nrows, users, other), jnp.float32),
        in_specs=[pl.BlockSpec(memory_space=pltpu.SMEM), pl.BlockSpec((users, items // nrows), lambda g: (0, g))],
        out_specs=pl.BlockSpec((1, users, other), lambda g: (g, 0, 0)),
        cost_estimate=pl.CostEstimate(flops=users * items, bytes_accessed=8 * users * items, transcendentals=0),
        name="mask_rest",
    )(block_mask, slab)


def shards(slab, block_mask):
    ncols = lax.axis_size("col")
    nrows = lax.axis_size("row")
    r = lax.axis_index("row")
    c = lax.axis_index("col")
    pair = ncols // nrows
    total_users = slab.shape[0] * ncols * nrows
    high = dict(precision=lax.Precision.HIGH, preferred_element_type=jnp.float32)
    over_users = (((0,), (0,)), ((), ()))

    band = band_columns(slab, block_mask, ncols)
    rest = other_columns(slab, block_mask, ncols, nrows)
    bands = lax.all_gather(band, "row", axis=0, tiled=True)

    upper = lax.dynamic_slice_in_dim(bands, BLK * r, BLK, 1)
    lower = lax.dynamic_slice_in_dim(bands, BLK * (ncols - 1 - r), BLK, 1)
    both = lax.dot_general(jnp.concatenate([lower, upper], axis=1), bands, over_users, **high)
    padded = jnp.concatenate([jnp.zeros((BLK, BLK * ncols), jnp.float32), both[BLK:]], axis=1)
    moved = lax.dynamic_slice_in_dim(padded, BLK * r, BLK * (ncols + 1), 1)
    long = jnp.concatenate([both[:BLK], jnp.zeros((BLK, BLK), jnp.float32)], axis=1)
    lane = lax.broadcasted_iota(jnp.int32, moved.shape, 1)
    packed = jnp.where(lane < BLK * (ncols - r), long, moved)
    pieces = lax.all_to_all(packed, "col", split_axis=0, concat_axis=0, tiled=True)
    mine = jnp.sum(pieces.reshape(ncols, BLK // ncols, -1), axis=0) / total_users
    mine, rest = lax.optimization_barrier((mine, rest))
    panel = lax.all_gather(mine, ("row", "col"), axis=0, tiled=True)

    others = lax.all_to_all(rest, "row", split_axis=0, concat_axis=0, tiled=True)
    others = others.reshape(-1, others.shape[-1])
    partial = lax.dot_general(bands, others, over_users, **high)
    panel, partial = lax.optimization_barrier((panel, partial))
    strip = lax.psum_scatter(partial, "col", scatter_dimension=0, tiled=True)

    place = jnp.stack([r, c]).astype(jnp.int32)
    block, piece = chol_piece(panel, place, BLK * ncols, BLK * pair)
    strip, block, piece = lax.optimization_barrier((strip, block, piece))
    half = strip.shape[1] // pair
    odd = c % 2
    own = lax.dynamic_slice_in_dim(strip, half * odd, half, 1)
    far = lax.dynamic_slice_in_dim(strip, half * (1 - odd), half, 1)
    at = [(i, j) for i in range(nrows) for j in range(ncols)]
    to = lambda i, j: i * ncols + j
    own = lax.ppermute(own, ("row", "col"), [(to(i, j), to(j // 2, 2 * i + j % 2)) for i, j in at])
    far = lax.ppermute(far, ("row", "col"), [(to(i, j), to(j // 2, 2 * i + 1 - j % 2)) for i, j in at])
    items = jnp.where(odd == 0, jnp.concatenate([own, far]), jnp.concatenate([far, own])) / total_users
    return (jnp.concatenate([block, items], axis=1), piece)


def solution(mesh):
    placed = (P(("row", "col"), None), P(("row", "col"), None))
    return jax.shard_map(
        shards,
        mesh=mesh,
        in_specs=placed,
        out_specs=(P("row", "col"), P("row", "col")),
        check_vma=False,
    )
```

```python
import functools

import jax
import jax.numpy as jnp
from jax import lax
from jax.experimental import pallas as pl
from jax.experimental.pallas import tpu as pltpu
from jax.sharding import PartitionSpec as P

BLK = 128
SHIFT_NUM = 2


def diag128(F, beside=lambda t: None):
    S = (8, 128)
    lane = lax.broadcasted_iota(jnp.int32, S, 1)
    subl = lax.broadcasted_iota(jnp.int32, S, 0)
    F = list(F)
    Ws = []
    onehot = [jnp.where(subl == k, 1.0, 0.0) for k in range(8)]
    n = len(F)
    spread = lambda x, at: [jnp.broadcast_to(x[:, at + k:at + k + 1], S) for k in range(8)]
    D = spread(F[0], 0)
    for t in range(n):
        b = 8 * t
        inblk = (lane >= b) & (lane < b + 8)
        X = jnp.where(inblk, jnp.where(lane - b == subl, 1.0, 0.0), F[t])
        if t + 1 < n:
            first = spread(F[t + 1], b)
            B = list(first)
            N = spread(F[t + 1], b + 8)
        C = {}
        for k in range(8):
            for s in range(t + 2, n):
                C[s, k] = jnp.broadcast_to(F[s][:, b + k:b + k + 1], S)
        G = jnp.zeros(S, jnp.float32)
        for k in range(8):
            d = jnp.broadcast_to(D[k][k:k + 1], S)
            rs = lax.rsqrt(d)
            inv = rs * rs
            g = D[k] - onehot[k]
            xk = jnp.broadcast_to(X[k:k + 1], S)
            G = jnp.where(subl == k, xk * rs, G)
            X = X - g * (xk * inv)
            for m in range(k + 1, 8):
                f = jnp.broadcast_to(D[m][k:k + 1], S) * inv
                D[m] = D[m] - g * f
                if t + 1 < n:
                    B[m] = B[m] - B[k] * f
            if t + 1 < n:
                y = B[k] * inv
                N = [N[m] - B[k] * jnp.broadcast_to(y[m:m + 1], S) for m in range(8)]
        Ws.append(jnp.where(lane < b + 8, G, 0.0))
        if t + 1 < n:
            V = [jnp.broadcast_to(X[k:k + 1], S) for k in range(8)]
            for s in range(t + 1, n):
                f = jnp.where(inblk, 0.0, F[s])
                for k in range(8):
                    f = f - (first[k] if s == t + 1 else C[s, k]) * V[k]
                F[s] = f
            D = N
        beside(t)
    return Ws


def split(x, n):
    parts = []
    for i in range(n):
        h = x.astype(jnp.bfloat16)
        parts.append(h)
        if i + 1 < n:
            x = x - h.astype(jnp.float32)
    return parts

PAIRS = {2: [(0, 0), (0, 1), (1, 0)], 3: [(0, 0), (0, 1), (1, 0), (0, 2), (1, 1), (2, 0)]}

def dot_nt(a, b):
    pairs = PAIRS[len(a)]
    x = jnp.concatenate([a[i] for i, _ in pairs], axis=1)
    y = jnp.concatenate([b[j] for _, j in pairs], axis=1)
    return lax.dot_general(x, y, (((1,), (1,)), ((), ())), preferred_element_type=jnp.float32)

BT = 512


def chol_kernel(nparts, place_ref, packed_ref, band_ref, out_ref, a_ref, *scratch):
    Ls = scratch[:nparts]
    P, Q, W, sems = scratch[nparts:]
    n = a_ref.shape[0]
    nb = n // BLK
    np2 = n // 256
    r = place_ref[0]
    c = place_ref[1]

    copies = []
    for i in range(nb):
        src = min(i, nb - 1 - i)
        first = 0 if 2 * i >= nb else BLK * (nb - i)
        copies.append(
            pltpu.make_async_copy(
                packed_ref.at[pl.ds(BLK * src, BLK), pl.ds(first, BLK * (i + 1))],
                a_ref.at[pl.ds(BLK * i, BLK), pl.ds(0, BLK * (i + 1))],
                sems.at[i],
            )
        )
    for copy in copies:
        copy.start()

    def zero(i, _):
        at = pl.ds(pl.multiple_of(i * 256, 256), 256)
        for L in Ls:
            L[at, :] = jnp.zeros((256, n), L.dtype)
        Q[at, :] = jnp.zeros((256, 256), jnp.float32)
        return 0

    lax.fori_loop(0, np2, zero, 0)
    out_ref[...] = jnp.zeros(out_ref.shape, jnp.float32)
    for copy in copies:
        copy.wait()

    for q in range(2):
        i = 2 * r + q
        rows_i = pl.multiple_of(i * BLK, BLK)
        cols_c = pl.multiple_of(c * BLK, BLK)

        @pl.when(c <= i)
        def _():
            band_ref[q * BLK:(q + 1) * BLK, :] = a_ref[pl.ds(rows_i, BLK), pl.ds(cols_c, BLK)]

        @pl.when(c > i)
        def _():
            band_ref[q * BLK:(q + 1) * BLK, :] = a_ref[pl.ds(cols_c, BLK), pl.ds(rows_i, BLK)].T

    row_of = lax.broadcasted_iota(jnp.int32, (BLK, BLK), 0)
    col_of = lax.broadcasted_iota(jnp.int32, (BLK, BLK), 1)
    shift = jnp.where(row_of == col_of, SHIFT_NUM / 4.0, 0.0)

    def column(jj, _):
        J2 = jj // 2
        h = jj % 2
        base = pl.multiple_of(J2 * 256, 256)
        here = pl.multiple_of(jj * 128, 128)
        first = base // BT

        @pl.when(jj == 0)
        def _():
            def rows(i, _):
                at = pl.ds(pl.multiple_of(i * BT, BT), BT)
                P[at, :] = a_ref[at, :256]
                return 0
            lax.fori_loop(0, n // BT, rows, 0)

        @pl.when((h == 0) & (jj > 0))
        def _():
            ks = pl.ds(pl.multiple_of(base - 256, 256), 256)
            def rows(i, _):
                at = pl.ds(pl.multiple_of(i * BT, BT), BT)
                P[at, :] = a_ref[at, pl.ds(base, 256)] + Q[at, :] - dot_nt([L[at, ks] for L in Ls], [L[pl.ds(base, 256), ks] for L in Ls])
                Q[at, :] = jnp.zeros((BT, 256), jnp.float32)
                return 0
            lax.fori_loop(first, n // BT, rows, 0)

        @pl.when(h == 1)
        def _():
            prev = pl.ds(pl.multiple_of(here - 128, 128), 128)
            def rows(i, _):
                at = pl.ds(pl.multiple_of(i * BT, BT), BT)
                P[at, :128] = P[at, 128:] - dot_nt([L[at, prev] for L in Ls], [L[pl.ds(here, 128), prev] for L in Ls])
                return 0
            lax.fori_loop(first, n // BT, rows, 0)

        units = (np2 // 2 * (np2 // 2 - 1) + 1) // 2
        later = jnp.minimum(J2 + 1, np2 - 1)
        deep = jnp.maximum(J2, 1)
        def unit(u):
            at = units * h + u
            real = at < J2 * (np2 - 1 - J2)
            i = J2 + 1 + at // deep
            src = pl.multiple_of(jnp.where(real, i, 0) * 256, 256)
            dst = pl.multiple_of(jnp.where(real, i, np2) * 256, 256)
            ks = pl.ds(pl.multiple_of(jnp.where(real, at % deep, 0) * 256, 256), 256)
            Q[pl.ds(dst, 256), :] -= dot_nt([L[pl.ds(src, 256), ks] for L in Ls], [L[pl.ds(pl.multiple_of(later * 256, 256), 256), ks] for L in Ls])
        def beside(t):
            if t % 2 == 0 and t // 2 < units:
                unit(t // 2)
        P[pl.ds(here, BLK), :BLK] += shift
        ws = diag128([P[pl.ds(pl.multiple_of(here + 8 * s, 8), 8), :128] for s in range(16)], beside)
        for s in range(16):
            W[8 * s:8 * s + 8, :] = ws[s]
        w = split(W[...], 3)
        def rows(i, _):
            at = pl.ds(pl.multiple_of(i * BT, BT), BT)
            l = dot_nt(split(P[at, :128], 3), w)
            for L, part in zip(Ls, split(l, nparts)):
                L[at, pl.ds(here, 128)] = part
            P[at, :128] = l
            return 0
        lax.fori_loop(first, n // BT, rows, 0)

        @pl.when(jj == c)
        def _():
            rows = out_ref.shape[0]
            mine = P[pl.ds(pl.multiple_of(r * rows, rows), rows), :128]
            row = lax.broadcasted_iota(jnp.int32, mine.shape, 0) + r * rows
            col = lax.broadcasted_iota(jnp.int32, mine.shape, 1) + here
            out_ref[...] = jnp.where(row >= col, mine, 0.0)
        return 0
    lax.fori_loop(0, n // 128, column, 0)


def chol_piece(packed, place, n, rows, nparts=3):
    nb = n // BLK
    flat = jax.ShapeDtypeStruct((rows, BLK), jnp.float32)
    vmem = pl.BlockSpec(memory_space=pltpu.VMEM)
    return pl.pallas_call(
        functools.partial(chol_kernel, nparts),
        out_shape=(flat, flat),
        in_specs=[pl.BlockSpec(memory_space=pltpu.SMEM), pl.BlockSpec(memory_space=pl.ANY)],
        out_specs=(vmem, vmem),
        scratch_shapes=[pltpu.VMEM((n, n), jnp.float32)]
        + [pltpu.VMEM((n, n), jnp.bfloat16)] * nparts
        + [pltpu.VMEM((n, 256), jnp.float32), pltpu.VMEM((n + 256, 256), jnp.float32), pltpu.VMEM((BLK, BLK), jnp.float32), pltpu.SemaphoreType.DMA((nb,))],
        compiler_params=pltpu.CompilerParams(vmem_limit_bytes=56 * 2**20),
        cost_estimate=pl.CostEstimate(flops=2 * n * n * n, bytes_accessed=300 * 2**20, transcendentals=n),
        name="factor",
    )(place, packed)


def band_kernel(keep_ref, slab_ref, band_ref, got, sems):
    ncols = band_ref.shape[1] // BLK
    step = slab_ref.shape[1] // ncols
    copies = [
        pltpu.make_async_copy(slab_ref.at[:, pl.ds(c * step, BLK)], got.at[:, pl.ds(c * BLK, BLK)], sems.at[c])
        for c in range(ncols)
    ]
    for copy in copies:
        copy.start()
    for c, copy in enumerate(copies):
        copy.wait()
        at = slice(c * BLK, (c + 1) * BLK)
        band_ref[:, at] = got[:, at] * keep_ref[0, c * step // BLK].astype(jnp.float32)


def band_columns(slab, block_mask, ncols):
    users = slab.shape[0]
    return pl.pallas_call(
        band_kernel,
        out_shape=jax.ShapeDtypeStruct((users, BLK * ncols), jnp.float32),
        in_specs=[pl.BlockSpec(memory_space=pltpu.SMEM), pl.BlockSpec(memory_space=pl.ANY)],
        out_specs=pl.BlockSpec(memory_space=pltpu.VMEM),
        scratch_shapes=[pltpu.VMEM((users, BLK * ncols), jnp.float32), pltpu.SemaphoreType.DMA((ncols,))],
        name="mask_band",
    )(block_mask, slab)


def rest_kernel(pair, keep_ref, slab_ref, rest_ref):
    g = pl.program_id(0)
    blocks = slab_ref.shape[1] // BLK
    per = blocks // pair
    to = 0
    for b in range(blocks):
        if b % per:
            keep = keep_ref[0, g * blocks + b].astype(jnp.float32)
            rest_ref[0, :, to:to + BLK] = slab_ref[:, b * BLK:(b + 1) * BLK] * keep
            to += BLK


def other_columns(slab, block_mask, ncols, nrows):
    users, items = slab.shape
    pair = ncols // nrows
    other = items // nrows - pair * BLK
    return pl.pallas_call(
        functools.partial(rest_kernel, pair),
        grid=(nrows,),
        out_shape=jax.ShapeDtypeStruct((nrows, users, other), jnp.float32),
        in_specs=[pl.BlockSpec(memory_space=pltpu.SMEM), pl.BlockSpec((users, items // nrows), lambda g: (0, g))],
        out_specs=pl.BlockSpec((1, users, other), lambda g: (g, 0, 0)),
        cost_estimate=pl.CostEstimate(flops=users * items, bytes_accessed=8 * users * items, transcendentals=0),
        name="mask_rest",
    )(block_mask, slab)


def shards(slab, block_mask):
    ncols = lax.axis_size("col")
    nrows = lax.axis_size("row")
    r = lax.axis_index("row")
    c = lax.axis_index("col")
    pair = ncols // nrows
    total_users = slab.shape[0] * ncols * nrows
    high = dict(precision=lax.Precision.HIGH, preferred_element_type=jnp.float32)
    over_users = (((0,), (0,)), ((), ()))

    band = band_columns(slab, block_mask, ncols)
    rest = other_columns(slab, block_mask, ncols, nrows)
    bands = lax.all_gather(band, "row", axis=0, tiled=True)

    upper = lax.dynamic_slice_in_dim(bands, BLK * r, BLK, 1)
    lower = lax.dynamic_slice_in_dim(bands, BLK * (ncols - 1 - r), BLK, 1)
    both = lax.dot_general(jnp.concatenate([lower, upper], axis=1), bands, over_users, **high)
    padded = jnp.concatenate([jnp.zeros((BLK, BLK * ncols), jnp.float32), both[BLK:]], axis=1)
    moved = lax.dynamic_slice_in_dim(padded, BLK * r, BLK * (ncols + 1), 1)
    long = jnp.concatenate([both[:BLK], jnp.zeros((BLK, BLK), jnp.float32)], axis=1)
    lane = lax.broadcasted_iota(jnp.int32, moved.shape, 1)
    packed = jnp.where(lane < BLK * (ncols - r), long, moved)
    pieces = lax.all_to_all(packed, "col", split_axis=0, concat_axis=0, tiled=True)
    mine = jnp.sum(pieces.reshape(ncols, BLK // ncols, -1), axis=0) / total_users
    mine, rest = lax.optimization_barrier((mine, rest))
    panel = lax.all_gather(mine, ("row", "col"), axis=0, tiled=True)

    others = lax.all_to_all(rest, "row", split_axis=0, concat_axis=0, tiled=True)
    others = others.reshape(-1, others.shape[-1])
    partial = lax.dot_general(bands, others, over_users, **high)
    panel, partial = lax.optimization_barrier((panel, partial))
    strip = lax.psum_scatter(partial, "col", scatter_dimension=0, tiled=True)

    place = jnp.stack([r, c]).astype(jnp.int32)
    block, piece = chol_piece(panel, place, BLK * ncols, BLK * pair)
    strip, block, piece = lax.optimization_barrier((strip, block, piece))
    half = strip.shape[1] // pair
    odd = c % 2
    own = lax.dynamic_slice_in_dim(strip, half * odd, half, 1)
    far = lax.dynamic_slice_in_dim(strip, half * (1 - odd), half, 1)
    at = [(i, j) for i in range(nrows) for j in range(ncols)]
    to = lambda i, j: i * ncols + j
    own = lax.ppermute(own, ("row", "col"), [(to(i, j), to(j // 2, 2 * i + j % 2)) for i, j in at])
    far = lax.ppermute(far, ("row", "col"), [(to(i, j), to(j // 2, 2 * i + 1 - j % 2)) for i, j in at])
    items = jnp.where(odd == 0, jnp.concatenate([own, far]), jnp.concatenate([far, own])) / total_users
    return (jnp.concatenate([block, items], axis=1), piece)


def solution(mesh):
    placed = (P(("row", "col"), None), P(("row", "col"), None))
    return jax.shard_map(
        shards,
        mesh=mesh,
        in_specs=placed,
        out_specs=(P("row", "col"), P("row", "col")),
        check_vma=False,
    )
```

```python
import functools

import jax
import jax.numpy as jnp
from jax import lax
from jax.experimental import pallas as pl
from jax.experimental.pallas import tpu as pltpu
from jax.sharding import Mesh
from jax.sharding import PartitionSpec as P

BLK = 128
SHIFT_NUM = 2


def diag128(F, beside=lambda t: None):
    S = (8, 128)
    lane = lax.broadcasted_iota(jnp.int32, S, 1)
    subl = lax.broadcasted_iota(jnp.int32, S, 0)
    F = list(F)
    Ws = []
    onehot = [jnp.where(subl == k, 1.0, 0.0) for k in range(8)]
    n = len(F)
    spread = lambda x, at: [jnp.broadcast_to(x[:, at + k:at + k + 1], S) for k in range(8)]
    D = spread(F[0], 0)
    for t in range(n):
        b = 8 * t
        inblk = (lane >= b) & (lane < b + 8)
        X = jnp.where(inblk, jnp.where(lane - b == subl, 1.0, 0.0), F[t])
        if t + 1 < n:
            first = spread(F[t + 1], b)
            B = list(first)
            N = spread(F[t + 1], b + 8)
        C = {}
        for k in range(8):
            for s in range(t + 2, n):
                C[s, k] = jnp.broadcast_to(F[s][:, b + k:b + k + 1], S)
        G = jnp.zeros(S, jnp.float32)
        for k in range(8):
            d = jnp.broadcast_to(D[k][k:k + 1], S)
            rs = lax.rsqrt(d)
            inv = rs * rs
            g = D[k] - onehot[k]
            xk = jnp.broadcast_to(X[k:k + 1], S)
            G = jnp.where(subl == k, xk * rs, G)
            X = X - g * (xk * inv)
            for m in range(k + 1, 8):
                f = jnp.broadcast_to(D[m][k:k + 1], S) * inv
                D[m] = D[m] - g * f
                if t + 1 < n:
                    B[m] = B[m] - B[k] * f
            if t + 1 < n:
                y = B[k] * inv
                N = [N[m] - B[k] * jnp.broadcast_to(y[m:m + 1], S) for m in range(8)]
        Ws.append(jnp.where(lane < b + 8, G, 0.0))
        if t + 1 < n:
            V = [jnp.broadcast_to(X[k:k + 1], S) for k in range(8)]
            for s in range(t + 1, n):
                f = jnp.where(inblk, 0.0, F[s])
                for k in range(8):
                    f = f - (first[k] if s == t + 1 else C[s, k]) * V[k]
                F[s] = f
            D = N
        beside(t)
    return Ws


def split(x, n):
    parts = []
    for i in range(n):
        h = x.astype(jnp.bfloat16)
        parts.append(h)
        if i + 1 < n:
            x = x - h.astype(jnp.float32)
    return parts

PAIRS = {2: [(0, 0), (0, 1), (1, 0)], 3: [(0, 0), (0, 1), (1, 0), (0, 2), (1, 1), (2, 0)]}

def dot_nt(a, b):
    pairs = PAIRS[len(a)]
    x = jnp.concatenate([a[i] for i, _ in pairs], axis=1)
    y = jnp.concatenate([b[j] for _, j in pairs], axis=1)
    return lax.dot_general(x, y, (((1,), (1,)), ((), ())), preferred_element_type=jnp.float32)

BT = 512


def chol_kernel(nparts, place_ref, packed_ref, band_ref, out_ref, a_ref, *scratch):
    Ls = scratch[:nparts]
    P, Q, W, sems = scratch[nparts:]
    n = a_ref.shape[0]
    nb = n // BLK
    np2 = n // 256
    r = place_ref[0]
    c = place_ref[1]

    early, late = [], []
    for i in range(nb):
        src = min(i, nb - 1 - i)
        first = 0 if 2 * i >= nb else BLK * (nb - i)
        for group, lo, hi in ((early, 0, min(2, i + 1)), (late, 2, i + 1)):
            if hi > lo:
                group.append(
                    pltpu.make_async_copy(
                        packed_ref.at[pl.ds(BLK * src, BLK), pl.ds(first + BLK * lo, BLK * (hi - lo))],
                        a_ref.at[pl.ds(BLK * i, BLK), pl.ds(BLK * lo, BLK * (hi - lo))],
                        sems.at[len(early) + len(late)],
                    )
                )
    for copy in early + late:
        copy.start()

    def zero(i, _):
        at = pl.ds(pl.multiple_of(i * 256, 256), 256)
        Q[at, :] = jnp.zeros((256, 256), jnp.float32)
        return 0

    lax.fori_loop(0, np2, zero, 0)
    out_ref[...] = jnp.zeros(out_ref.shape, jnp.float32)
    for copy in early:
        copy.wait()

    row_of = lax.broadcasted_iota(jnp.int32, (BLK, BLK), 0)
    col_of = lax.broadcasted_iota(jnp.int32, (BLK, BLK), 1)
    shift = jnp.where(row_of == col_of, SHIFT_NUM / 4.0, 0.0)

    def column(jj, _):
        J2 = jj // 2
        h = jj % 2
        base = pl.multiple_of(J2 * 256, 256)
        here = pl.multiple_of(jj * 128, 128)
        first = base // BT

        @pl.when(jj == 0)
        def _():
            def rows(i, _):
                at = pl.ds(pl.multiple_of(i * BT, BT), BT)
                P[at, :] = a_ref[at, :256]
                return 0
            lax.fori_loop(0, n // BT, rows, 0)

        @pl.when(jj == 1)
        def _():
            for copy in late:
                copy.wait()

        @pl.when((h == 0) & (jj > 0))
        def _():
            ks = pl.ds(pl.multiple_of(base - 256, 256), 256)
            def rows(i, _):
                at = pl.ds(pl.multiple_of(i * BT, BT), BT)
                P[at, :] = a_ref[at, pl.ds(base, 256)] + Q[at, :] - dot_nt([L[at, ks] for L in Ls], [L[pl.ds(base, 256), ks] for L in Ls])
                Q[at, :] = jnp.zeros((BT, 256), jnp.float32)
                return 0
            lax.fori_loop(first, n // BT, rows, 0)

        @pl.when(h == 1)
        def _():
            prev = pl.ds(pl.multiple_of(here - 128, 128), 128)
            def rows(i, _):
                at = pl.ds(pl.multiple_of(i * BT, BT), BT)
                P[at, :128] = P[at, 128:] - dot_nt([L[at, prev] for L in Ls], [L[pl.ds(here, 128), prev] for L in Ls])
                return 0
            lax.fori_loop(first, n // BT, rows, 0)

        units = (np2 // 2 * (np2 // 2 - 1) + 1) // 2
        later = jnp.minimum(J2 + 1, np2 - 1)
        deep = jnp.maximum(J2, 1)
        def unit(u):
            at = units * h + u
            real = at < J2 * (np2 - 1 - J2)
            i = J2 + 1 + at // deep
            src = pl.multiple_of(jnp.where(real, i, 0) * 256, 256)
            dst = pl.multiple_of(jnp.where(real, i, np2) * 256, 256)
            ks = pl.ds(pl.multiple_of(jnp.where(real, at % deep, 0) * 256, 256), 256)
            Q[pl.ds(dst, 256), :] -= dot_nt([L[pl.ds(src, 256), ks] for L in Ls], [L[pl.ds(pl.multiple_of(later * 256, 256), 256), ks] for L in Ls])
        def beside(t):
            if t % 2 == 0 and t // 2 < units:
                unit(t // 2)
        P[pl.ds(here, BLK), :BLK] += shift
        ws = diag128([P[pl.ds(pl.multiple_of(here + 8 * s, 8), 8), :128] for s in range(16)], beside)
        for s in range(16):
            W[8 * s:8 * s + 8, :] = ws[s]
        w = split(W[...], 3)
        def rows(i, _):
            at = pl.ds(pl.multiple_of(i * BT, BT), BT)
            l = dot_nt(split(P[at, :128], 3), w)
            for L, part in zip(Ls, split(l, nparts)):
                L[at, pl.ds(here, 128)] = part
            P[at, :128] = l
            return 0
        lax.fori_loop(first, n // BT, rows, 0)

        @pl.when(jj == c)
        def _():
            rows = out_ref.shape[0]
            mine = P[pl.ds(pl.multiple_of(r * rows, rows), rows), :128]
            row = lax.broadcasted_iota(jnp.int32, mine.shape, 0) + r * rows
            col = lax.broadcasted_iota(jnp.int32, mine.shape, 1) + here
            out_ref[...] = jnp.where(row >= col, mine, 0.0)
        return 0
    lax.fori_loop(0, n // 128, column, 0)

    for q in range(2):
        i = 2 * r + q
        rows_i = pl.multiple_of(i * BLK, BLK)
        cols_c = pl.multiple_of(c * BLK, BLK)

        @pl.when(c <= i)
        def _():
            band_ref[q * BLK:(q + 1) * BLK, :] = a_ref[pl.ds(rows_i, BLK), pl.ds(cols_c, BLK)]

        @pl.when(c > i)
        def _():
            band_ref[q * BLK:(q + 1) * BLK, :] = a_ref[pl.ds(cols_c, BLK), pl.ds(rows_i, BLK)].T


def chol_piece(packed, place, n, rows, nparts=3):
    nb = n // BLK
    flat = jax.ShapeDtypeStruct((rows, BLK), jnp.float32)
    vmem = pl.BlockSpec(memory_space=pltpu.VMEM)
    return pl.pallas_call(
        functools.partial(chol_kernel, nparts),
        out_shape=(flat, flat),
        in_specs=[pl.BlockSpec(memory_space=pltpu.SMEM), pl.BlockSpec(memory_space=pl.ANY)],
        out_specs=(vmem, vmem),
        scratch_shapes=[pltpu.VMEM((n, n), jnp.float32)]
        + [pltpu.VMEM((n, n), jnp.bfloat16)] * nparts
        + [pltpu.VMEM((n, 256), jnp.float32), pltpu.VMEM((n + 256, 256), jnp.float32), pltpu.VMEM((BLK, BLK), jnp.float32), pltpu.SemaphoreType.DMA((2 * nb,))],
        compiler_params=pltpu.CompilerParams(vmem_limit_bytes=56 * 2**20),
        cost_estimate=pl.CostEstimate(flops=2 * n * n * n, bytes_accessed=300 * 2**20, transcendentals=n),
        name="factor",
    )(place, packed)


def band_kernel(keep_ref, slab_ref, band_ref, got, sems):
    ncols = band_ref.shape[1] // BLK
    step = slab_ref.shape[1] // ncols
    copies = [
        pltpu.make_async_copy(slab_ref.at[:, pl.ds(c * step, BLK)], got.at[:, pl.ds(c * BLK, BLK)], sems.at[c])
        for c in range(ncols)
    ]
    for copy in copies:
        copy.start()
    for c, copy in enumerate(copies):
        copy.wait()
        at = slice(c * BLK, (c + 1) * BLK)
        band_ref[:, at] = got[:, at] * keep_ref[0, c * step // BLK].astype(jnp.float32)


def band_columns(slab, block_mask, ncols):
    users = slab.shape[0]
    return pl.pallas_call(
        band_kernel,
        out_shape=jax.ShapeDtypeStruct((users, BLK * ncols), jnp.float32),
        in_specs=[pl.BlockSpec(memory_space=pltpu.SMEM), pl.BlockSpec(memory_space=pl.ANY)],
        out_specs=pl.BlockSpec(memory_space=pltpu.VMEM),
        scratch_shapes=[pltpu.VMEM((users, BLK * ncols), jnp.float32), pltpu.SemaphoreType.DMA((ncols,))],
        name="mask_band",
    )(block_mask, slab)


def rest_kernel(pair, keep_ref, slab_ref, rest_ref):
    g = pl.program_id(0)
    blocks = slab_ref.shape[1] // BLK
    per = blocks // pair
    to = 0
    for b in range(blocks):
        if b % per:
            keep = keep_ref[0, g * blocks + b].astype(jnp.float32)
            rest_ref[0, :, to:to + BLK] = slab_ref[:, b * BLK:(b + 1) * BLK] * keep
            to += BLK


def other_columns(slab, block_mask, ncols, nrows):
    users, items = slab.shape
    pair = ncols // nrows
    other = items // nrows - pair * BLK
    return pl.pallas_call(
        functools.partial(rest_kernel, pair),
        grid=(nrows,),
        out_shape=jax.ShapeDtypeStruct((nrows, users, other), jnp.float32),
        in_specs=[pl.BlockSpec(memory_space=pltpu.SMEM), pl.BlockSpec((users, items // nrows), lambda g: (0, g))],
        out_specs=pl.BlockSpec((1, users, other), lambda g: (g, 0, 0)),
        cost_estimate=pl.CostEstimate(flops=users * items, bytes_accessed=8 * users * items, transcendentals=0),
        name="mask_rest",
    )(block_mask, slab)


def shards(slab, block_mask):
    z, k, y, x = (lax.axis_index(axis) for axis in ("z", "k", "y", "x"))
    groups = lax.axis_size("y") * lax.axis_size("k")
    ncols = lax.axis_size("z") * lax.axis_size("x")
    g = lax.axis_size("k") * y + k
    pair = ncols // groups
    total_users = slab.shape[0] * ncols * groups
    high = dict(precision=lax.Precision.HIGH, preferred_element_type=jnp.float32)
    over_users = (((0,), (0,)), ((), ()))

    band = band_columns(slab, block_mask, ncols)
    rest = other_columns(slab, block_mask, ncols, groups)
    bands = lax.all_gather(band, ("y", "k"), axis=0, tiled=True)

    upper = lax.dynamic_slice_in_dim(bands, BLK * g, BLK, 1)
    lower = lax.dynamic_slice_in_dim(bands, BLK * (ncols - 1 - g), BLK, 1)
    both = lax.dot_general(jnp.concatenate([lower, upper], axis=1), bands, over_users, **high)
    padded = jnp.concatenate([jnp.zeros((BLK, BLK * ncols), jnp.float32), both[BLK:]], axis=1)
    moved = lax.dynamic_slice_in_dim(padded, BLK * g, BLK * (ncols + 1), 1)
    long = jnp.concatenate([both[:BLK], jnp.zeros((BLK, BLK), jnp.float32)], axis=1)
    lane = lax.broadcasted_iota(jnp.int32, moved.shape, 1)
    packed = jnp.where(lane < BLK * (ncols - g), long, moved)
    pieces = lax.all_to_all(packed, ("z", "x"), split_axis=0, concat_axis=0, tiled=True)
    mine = jnp.sum(pieces.reshape(ncols, BLK // ncols, -1), axis=0) / total_users
    mine, rest = lax.optimization_barrier((mine, rest))
    panel = lax.all_gather(mine, ("y", "k", "z", "x"), axis=0, tiled=True)

    others = lax.all_to_all(rest, ("y", "k"), split_axis=0, concat_axis=0, tiled=True)
    others = others.reshape(-1, others.shape[-1])
    partial = lax.dot_general(bands, others, over_users, **high)
    panel, partial = lax.optimization_barrier((panel, partial))
    strip = lax.psum_scatter(partial, ("z", "x"), scatter_dimension=0, tiled=True)

    place = jnp.stack([lax.axis_size("k") * z + k, lax.axis_size("x") * y + x]).astype(jnp.int32)
    block, piece = chol_piece(panel, place, BLK * ncols, BLK * pair)
    strip, block, piece = lax.optimization_barrier((strip, block, piece))
    half = strip.shape[1] // pair
    odd = x % 2
    own = lax.dynamic_slice_in_dim(strip, half * odd, half, 1)
    far = lax.dynamic_slice_in_dim(strip, half * (1 - odd), half, 1)
    nx = lax.axis_size("x")
    at = [(i, j) for i in range(lax.axis_size("k")) for j in range(nx)]
    to = lambda i, j: i * nx + j
    own = lax.ppermute(own, ("k", "x"), [(to(i, j), to(j // 2, 2 * i + j % 2)) for i, j in at])
    far = lax.ppermute(far, ("k", "x"), [(to(i, j), to(j // 2, 2 * i + 1 - j % 2)) for i, j in at])
    items = jnp.where(odd == 0, jnp.concatenate([own, far]), jnp.concatenate([far, own])) / total_users
    return (jnp.concatenate([block, items], axis=1), piece)


def solution(mesh):
    rows, cols = mesh.devices.shape
    axes = ("z", "k", "y", "x")
    fine = Mesh(mesh.devices.reshape(rows // 2, 2, cols // 4, 4), axes)
    return jax.shard_map(
        shards,
        mesh=fine,
        in_specs=(P(axes, None), P(axes, None)),
        out_specs=(P(("z", "k"), ("y", "x")), P(("z", "k"), ("y", "x"))),
        check_vma=False,
    )
```

```python
import functools

import jax
import jax.numpy as jnp
from jax import lax
from jax.experimental import pallas as pl
from jax.experimental.pallas import tpu as pltpu
from jax.sharding import Mesh
from jax.sharding import PartitionSpec as P

BLK = 128
SHIFT_NUM = 2


def diag128(F, beside=lambda t: None):
    S = (8, 128)
    lane = lax.broadcasted_iota(jnp.int32, S, 1)
    subl = lax.broadcasted_iota(jnp.int32, S, 0)
    F = list(F)
    Ws = []
    onehot = [jnp.where(subl == k, 1.0, 0.0) for k in range(8)]
    n = len(F)
    spread = lambda x, at: [jnp.broadcast_to(x[:, at + k:at + k + 1], S) for k in range(8)]
    D = spread(F[0], 0)
    for t in range(n):
        b = 8 * t
        inblk = (lane >= b) & (lane < b + 8)
        X = jnp.where(inblk, jnp.where(lane - b == subl, 1.0, 0.0), F[t])
        if t + 1 < n:
            first = spread(F[t + 1], b)
            B = list(first)
            N = spread(F[t + 1], b + 8)
        C = {}
        for k in range(8):
            for s in range(t + 2, n):
                C[s, k] = jnp.broadcast_to(F[s][:, b + k:b + k + 1], S)
        G = jnp.zeros(S, jnp.float32)
        for k in range(8):
            d = jnp.broadcast_to(D[k][k:k + 1], S)
            rs = lax.rsqrt(d)
            inv = 1.0 / d
            g = D[k] - onehot[k]
            xk = jnp.broadcast_to(X[k:k + 1], S)
            G = jnp.where(subl == k, xk * rs, G)
            X = X - g * (xk * inv)
            for m in range(k + 1, 8):
                f = jnp.broadcast_to(D[m][k:k + 1], S) * inv
                D[m] = D[m] - g * f
                if t + 1 < n:
                    B[m] = B[m] - B[k] * f
            if t + 1 < n:
                y = B[k] * inv
                N = [N[m] - B[k] * jnp.broadcast_to(y[m:m + 1], S) for m in range(8)]
        Ws.append(jnp.where(lane < b + 8, G, 0.0))
        if t + 1 < n:
            V = [jnp.broadcast_to(X[k:k + 1], S) for k in range(8)]
            for s in range(t + 1, n):
                f = jnp.where(inblk, 0.0, F[s])
                for k in range(8):
                    f = f - (first[k] if s == t + 1 else C[s, k]) * V[k]
                F[s] = f
            D = N
        beside(t)
    return Ws


def split(x, n):
    parts = []
    for i in range(n):
        h = x.astype(jnp.bfloat16)
        parts.append(h)
        if i + 1 < n:
            x = x - h.astype(jnp.float32)
    return parts

PAIRS = {2: [(0, 0), (0, 1), (1, 0)], 3: [(0, 0), (0, 1), (1, 0), (0, 2), (1, 1), (2, 0)]}

def dot_nt(a, b):
    pairs = PAIRS[len(a)]
    x = jnp.concatenate([a[i] for i, _ in pairs], axis=1)
    y = jnp.concatenate([b[j] for _, j in pairs], axis=1)
    return lax.dot_general(x, y, (((1,), (1,)), ((), ())), preferred_element_type=jnp.float32)

def dot_nt_narrow(a, b):
    rows = b[0].shape[0]
    x = jnp.concatenate([a[0], a[1]], axis=1)
    y = jnp.concatenate([jnp.concatenate([b[0], b[1]], axis=1), jnp.concatenate([b[1], b[0]], axis=1)], axis=0)
    u = lax.dot_general(x, y, (((1,), (1,)), ((), ())), preferred_element_type=jnp.float32)
    x = jnp.concatenate([a[0], a[2]], axis=1)
    y = jnp.concatenate([b[2], b[0]], axis=1)
    v = lax.dot_general(x, y, (((1,), (1,)), ((), ())), preferred_element_type=jnp.float32)
    return u[:, :rows] + (u[:, rows:] + v)


BT = 256


def each_tile(first, n, body):
    for f in range(n // BT):

        @pl.when(first == f)
        def _():
            for i in range(f, n // BT):
                body(i)


def chol_kernel(nparts, place_ref, packed_ref, band_ref, out_ref, a_ref, *scratch):
    Ls = scratch[:nparts]
    P, Q, W, sems = scratch[nparts:]
    n = a_ref.shape[0]
    nb = n // BLK
    np2 = n // 256
    r = place_ref[0]
    c = place_ref[1]

    early, late = [], []
    for i in range(nb):
        src = min(i, nb - 1 - i)
        first = 0 if 2 * i >= nb else BLK * (nb - i)
        for group, lo, hi in ((early, 0, min(2, i + 1)), (late, 2, i + 1)):
            if hi > lo:
                group.append(
                    pltpu.make_async_copy(
                        packed_ref.at[pl.ds(BLK * src, BLK), pl.ds(first + BLK * lo, BLK * (hi - lo))],
                        a_ref.at[pl.ds(BLK * i, BLK), pl.ds(BLK * lo, BLK * (hi - lo))],
                        sems.at[len(early) + len(late)],
                    )
                )
    for copy in early + late:
        copy.start()

    def zero(i, _):
        at = pl.ds(pl.multiple_of(i * 256, 256), 256)
        Q[at, :] = jnp.zeros((256, 256), jnp.float32)
        return 0

    lax.fori_loop(0, np2, zero, 0)
    out_ref[...] = jnp.zeros(out_ref.shape, jnp.float32)
    for copy in early:
        copy.wait()

    row_of = lax.broadcasted_iota(jnp.int32, (BLK, BLK), 0)
    col_of = lax.broadcasted_iota(jnp.int32, (BLK, BLK), 1)
    shift = jnp.where(row_of == col_of, SHIFT_NUM / 4.0, 0.0)

    def column(jj, _):
        J2 = jj // 2
        h = jj % 2
        base = pl.multiple_of(J2 * 256, 256)
        here = pl.multiple_of(jj * 128, 128)
        first = base // BT

        @pl.when(jj == 0)
        def _():
            def rows(i):
                at = pl.ds(i * BT, BT)
                P[at, :] = a_ref[at, :256]
            for i in range(n // BT):
                rows(i)

        @pl.when(jj == 1)
        def _():
            for copy in late:
                copy.wait()

        @pl.when((h == 0) & (jj > 0))
        def _():
            ks = pl.ds(pl.multiple_of(base - 256, 256), 256)
            def rows(i):
                at = pl.ds(i * BT, BT)
                P[at, :] = a_ref[at, pl.ds(base, 256)] + Q[at, :] - dot_nt([L[at, ks] for L in Ls], [L[pl.ds(base, 256), ks] for L in Ls])
                Q[at, :] = jnp.zeros((BT, 256), jnp.float32)
            each_tile(first, n, rows)

        @pl.when(h == 1)
        def _():
            prev = pl.ds(pl.multiple_of(here - 128, 128), 128)
            def rows(i):
                at = pl.ds(i * BT, BT)
                P[at, :128] = P[at, 128:] - dot_nt_narrow([L[at, prev] for L in Ls], [L[pl.ds(here, 128), prev] for L in Ls])
            each_tile(first, n, rows)

        units = (np2 // 2 * (np2 // 2 - 1) + 1) // 2
        later = jnp.minimum(J2 + 1, np2 - 1)
        deep = jnp.maximum(J2, 1)
        def unit(u):
            at = units * h + u
            real = at < J2 * (np2 - 1 - J2)
            i = J2 + 1 + at // deep
            src = pl.multiple_of(jnp.where(real, i, 0) * 256, 256)
            dst = pl.multiple_of(jnp.where(real, i, np2) * 256, 256)
            ks = pl.ds(pl.multiple_of(jnp.where(real, at % deep, 0) * 256, 256), 256)
            Q[pl.ds(dst, 256), :] -= dot_nt([L[pl.ds(src, 256), ks] for L in Ls], [L[pl.ds(pl.multiple_of(later * 256, 256), 256), ks] for L in Ls])
        def beside(t):
            if t % 2 == 0 and t // 2 < units:
                unit(t // 2)
        P[pl.ds(here, BLK), :BLK] += shift
        ws = diag128([P[pl.ds(pl.multiple_of(here + 8 * s, 8), 8), :128] for s in range(16)], beside)
        for s in range(16):
            W[8 * s:8 * s + 8, :] = ws[s]
        w = split(W[...], 3)
        def rows(i):
            at = pl.ds(i * BT, BT)
            l = dot_nt_narrow(split(P[at, :128], 3), w)
            for L, part in zip(Ls, split(l, nparts)):
                L[at, pl.ds(here, 128)] = part
            P[at, :128] = l
        each_tile(first, n, rows)

        @pl.when(jj == c)
        def _():
            rows = out_ref.shape[0]
            mine = P[pl.ds(pl.multiple_of(r * rows, rows), rows), :128]
            row = lax.broadcasted_iota(jnp.int32, mine.shape, 0) + r * rows
            col = lax.broadcasted_iota(jnp.int32, mine.shape, 1) + here
            out_ref[...] = jnp.where(row >= col, mine, 0.0)
        return 0
    lax.fori_loop(0, n // 128, column, 0)

    for q in range(2):
        i = 2 * r + q
        rows_i = pl.multiple_of(i * BLK, BLK)
        cols_c = pl.multiple_of(c * BLK, BLK)

        @pl.when(c <= i)
        def _():
            band_ref[q * BLK:(q + 1) * BLK, :] = a_ref[pl.ds(rows_i, BLK), pl.ds(cols_c, BLK)]

        @pl.when(c > i)
        def _():
            band_ref[q * BLK:(q + 1) * BLK, :] = a_ref[pl.ds(cols_c, BLK), pl.ds(rows_i, BLK)].T


def chol_piece(packed, place, n, rows, nparts=3):
    nb = n // BLK
    flat = jax.ShapeDtypeStruct((rows, BLK), jnp.float32)
    vmem = pl.BlockSpec(memory_space=pltpu.VMEM)
    return pl.pallas_call(
        functools.partial(chol_kernel, nparts),
        out_shape=(flat, flat),
        in_specs=[pl.BlockSpec(memory_space=pltpu.SMEM), pl.BlockSpec(memory_space=pl.ANY)],
        out_specs=(vmem, vmem),
        scratch_shapes=[pltpu.VMEM((n, n), jnp.float32)]
        + [pltpu.VMEM((n, n), jnp.bfloat16)] * nparts
        + [pltpu.VMEM((n, 256), jnp.float32), pltpu.VMEM((n + 256, 256), jnp.float32), pltpu.VMEM((BLK, BLK), jnp.float32), pltpu.SemaphoreType.DMA((2 * nb,))],
        compiler_params=pltpu.CompilerParams(vmem_limit_bytes=56 * 2**20),
        cost_estimate=pl.CostEstimate(flops=2 * n * n * n, bytes_accessed=300 * 2**20, transcendentals=n),
        name="factor",
    )(place, packed)


def band_kernel(keep_ref, slab_ref, band_ref, got, sems):
    ncols = band_ref.shape[1] // BLK
    step = slab_ref.shape[1] // ncols
    copies = [
        pltpu.make_async_copy(slab_ref.at[:, pl.ds(c * step, BLK)], got.at[:, pl.ds(c * BLK, BLK)], sems.at[c])
        for c in range(ncols)
    ]
    for copy in copies:
        copy.start()
    for c, copy in enumerate(copies):
        copy.wait()
        at = slice(c * BLK, (c + 1) * BLK)
        band_ref[:, at] = got[:, at] * keep_ref[0, c * step // BLK].astype(jnp.float32)


def band_columns(slab, block_mask, ncols):
    users = slab.shape[0]
    return pl.pallas_call(
        band_kernel,
        out_shape=jax.ShapeDtypeStruct((users, BLK * ncols), jnp.float32),
        in_specs=[pl.BlockSpec(memory_space=pltpu.SMEM), pl.BlockSpec(memory_space=pl.ANY)],
        out_specs=pl.BlockSpec(memory_space=pltpu.VMEM),
        scratch_shapes=[pltpu.VMEM((users, BLK * ncols), jnp.float32), pltpu.SemaphoreType.DMA((ncols,))],
        name="mask_band",
    )(block_mask, slab)


def rest_kernel(pair, keep_ref, slab_ref, rest_ref):
    g = pl.program_id(0)
    blocks = slab_ref.shape[1] // BLK
    per = blocks // pair
    to = 0
    for b in range(blocks):
        if b % per:
            keep = keep_ref[0, g * blocks + b].astype(jnp.float32)
            rest_ref[0, :, to:to + BLK] = slab_ref[:, b * BLK:(b + 1) * BLK] * keep
            to += BLK


def other_columns(slab, block_mask, ncols, nrows):
    users, items = slab.shape
    pair = ncols // nrows
    other = items // nrows - pair * BLK
    return pl.pallas_call(
        functools.partial(rest_kernel, pair),
        grid=(nrows,),
        out_shape=jax.ShapeDtypeStruct((nrows, users, other), jnp.float32),
        in_specs=[pl.BlockSpec(memory_space=pltpu.SMEM), pl.BlockSpec((users, items // nrows), lambda g: (0, g))],
        out_specs=pl.BlockSpec((1, users, other), lambda g: (g, 0, 0)),
        cost_estimate=pl.CostEstimate(flops=users * items, bytes_accessed=8 * users * items, transcendentals=0),
        name="mask_rest",
    )(block_mask, slab)


def shards(slab, block_mask):
    z, k, y, x = (lax.axis_index(axis) for axis in ("z", "k", "y", "x"))
    groups = lax.axis_size("y") * lax.axis_size("k")
    ncols = lax.axis_size("z") * lax.axis_size("x")
    g = lax.axis_size("k") * y + k
    pair = ncols // groups
    total_users = slab.shape[0] * ncols * groups
    high = dict(precision=lax.Precision.HIGH, preferred_element_type=jnp.float32)
    over_users = (((0,), (0,)), ((), ()))

    band = band_columns(slab, block_mask, ncols)
    rest = other_columns(slab, block_mask, ncols, groups)
    bands = lax.all_gather(band, ("y", "k"), axis=0, tiled=True)
    bands, rest = lax.optimization_barrier((bands, rest))

    upper = lax.dynamic_slice_in_dim(bands, BLK * g, BLK, 1)
    lower = lax.dynamic_slice_in_dim(bands, BLK * (ncols - 1 - g), BLK, 1)
    both = lax.dot_general(jnp.concatenate([lower, upper], axis=1), bands, over_users, **high)
    padded = jnp.concatenate([jnp.zeros((BLK, BLK * ncols), jnp.float32), both[BLK:]], axis=1)
    moved = lax.dynamic_slice_in_dim(padded, BLK * g, BLK * (ncols + 1), 1)
    long = jnp.concatenate([both[:BLK], jnp.zeros((BLK, BLK), jnp.float32)], axis=1)
    lane = lax.broadcasted_iota(jnp.int32, moved.shape, 1)
    packed = jnp.where(lane < BLK * (ncols - g), long, moved)
    pieces = lax.all_to_all(packed, ("z", "x"), split_axis=0, concat_axis=0, tiled=True)
    mine = jnp.sum(pieces.reshape(ncols, BLK // ncols, -1), axis=0) / total_users
    mine, rest = lax.optimization_barrier((mine, rest))
    panel = lax.all_gather(lax.all_gather(mine, "x", axis=0, tiled=True), ("y", "k", "z"), axis=0, tiled=True)

    others = lax.all_to_all(rest, ("y", "k"), split_axis=0, concat_axis=0, tiled=True)
    others = others.reshape(-1, others.shape[-1])
    partial = lax.dot_general(bands, others, over_users, **high)
    panel, partial = lax.optimization_barrier((panel, partial))
    strip = lax.psum_scatter(partial, ("z", "x"), scatter_dimension=0, tiled=True)

    place = jnp.stack([lax.axis_size("k") * z + k, lax.axis_size("x") * y + x]).astype(jnp.int32)
    block, piece = chol_piece(panel, place, BLK * ncols, BLK * pair)
    strip, block, piece = lax.optimization_barrier((strip, block, piece))
    half = strip.shape[1] // pair
    odd = x % 2
    own = lax.dynamic_slice_in_dim(strip, half * odd, half, 1)
    far = lax.dynamic_slice_in_dim(strip, half * (1 - odd), half, 1)
    nx = lax.axis_size("x")
    at = [(i, j) for i in range(lax.axis_size("k")) for j in range(nx)]
    to = lambda i, j: i * nx + j
    own = lax.ppermute(own, ("k", "x"), [(to(i, j), to(j // 2, 2 * i + j % 2)) for i, j in at])
    far = lax.ppermute(far, ("k", "x"), [(to(i, j), to(j // 2, 2 * i + 1 - j % 2)) for i, j in at])
    items = jnp.where(odd == 0, jnp.concatenate([own, far]), jnp.concatenate([far, own])) / total_users
    return (jnp.concatenate([block, items], axis=1), piece)


def solution(mesh):
    rows, cols = mesh.devices.shape
    axes = ("z", "k", "y", "x")
    fine = Mesh(mesh.devices.reshape(rows // 2, 2, cols // 4, 4), axes)
    return jax.shard_map(
        shards,
        mesh=fine,
        in_specs=(P(axes, None), P(axes, None)),
        out_specs=(P(("z", "k"), ("y", "x")), P(("z", "k"), ("y", "x"))),
        check_vma=False,
    )
```

```python
import functools

import jax
import jax.numpy as jnp
from jax import lax
from jax.experimental import pallas as pl
from jax.experimental.pallas import tpu as pltpu
from jax.sharding import Mesh
from jax.sharding import PartitionSpec as P

BLK = 128
SHIFT_NUM = 2


def diag128(F, beside=lambda t: None):
    S = (8, 128)
    lane = lax.broadcasted_iota(jnp.int32, S, 1)
    subl = lax.broadcasted_iota(jnp.int32, S, 0)
    F = list(F)
    Ws = []
    onehot = [jnp.where(subl == k, 1.0, 0.0) for k in range(8)]
    n = len(F)
    spread = lambda x, at: [jnp.broadcast_to(x[:, at + k:at + k + 1], S) for k in range(8)]
    D = spread(F[0], 0)
    for t in range(n):
        b = 8 * t
        inblk = (lane >= b) & (lane < b + 8)
        X = jnp.where(inblk, jnp.where(lane - b == subl, 1.0, 0.0), F[t])
        if t + 1 < n:
            first = spread(F[t + 1], b)
            B = list(first)
            N = spread(F[t + 1], b + 8)
        C = {}
        for k in range(8):
            for s in range(t + 2, n):
                C[s, k] = jnp.broadcast_to(F[s][:, b + k:b + k + 1], S)
        G = jnp.zeros(S, jnp.float32)
        for k in range(8):
            d = jnp.broadcast_to(D[k][k:k + 1], S)
            rs = lax.rsqrt(d)
            inv = 1.0 / d
            g = D[k] - onehot[k]
            xk = jnp.broadcast_to(X[k:k + 1], S)
            G = jnp.where(subl == k, xk * rs, G)
            X = X - g * (xk * inv)
            for m in range(k + 1, 8):
                f = jnp.broadcast_to(D[m][k:k + 1], S) * inv
                D[m] = D[m] - g * f
                if t + 1 < n:
                    B[m] = B[m] - B[k] * f
            if t + 1 < n:
                y = B[k] * inv
                N = [N[m] - B[k] * jnp.broadcast_to(y[m:m + 1], S) for m in range(8)]
        Ws.append(jnp.where(lane < b + 8, G, 0.0))
        if t + 1 < n:
            V = [jnp.broadcast_to(X[k:k + 1], S) for k in range(8)]
            for s in range(t + 1, n):
                f = jnp.where(inblk, 0.0, F[s])
                for k in range(8):
                    f = f - (first[k] if s == t + 1 else C[s, k]) * V[k]
                F[s] = f
            D = N
        beside(t)
    return Ws


def split(x, n):
    parts = []
    for i in range(n):
        h = x.astype(jnp.bfloat16)
        parts.append(h)
        if i + 1 < n:
            x = x - h.astype(jnp.float32)
    return parts

PAIRS = {2: [(0, 0), (0, 1), (1, 0)], 3: [(0, 0), (0, 1), (1, 0), (0, 2), (1, 1), (2, 0)]}

def dot_nt(a, b):
    pairs = PAIRS[len(a)]
    x = jnp.concatenate([a[i] for i, _ in pairs], axis=1)
    y = jnp.concatenate([b[j] for _, j in pairs], axis=1)
    return lax.dot_general(x, y, (((1,), (1,)), ((), ())), preferred_element_type=jnp.float32)

def dot_nt_narrow(a, b):
    rows = b[0].shape[0]
    x = jnp.concatenate([a[0], a[1]], axis=1)
    y = jnp.concatenate([jnp.concatenate([b[0], b[1]], axis=1), jnp.concatenate([b[1], b[0]], axis=1)], axis=0)
    u = lax.dot_general(x, y, (((1,), (1,)), ((), ())), preferred_element_type=jnp.float32)
    x = jnp.concatenate([a[0], a[2]], axis=1)
    y = jnp.concatenate([b[2], b[0]], axis=1)
    v = lax.dot_general(x, y, (((1,), (1,)), ((), ())), preferred_element_type=jnp.float32)
    return u[:, :rows] + (u[:, rows:] + v)


BT = 256


def each_tile(first, n, body):
    for f in range(n // BT):

        @pl.when(first == f)
        def _():
            for i in range(f, n // BT):
                body(i)


def chol_kernel(nparts, place_ref, packed_ref, band_ref, out_ref, a_ref, *scratch):
    Ls = scratch[:nparts]
    P, Q, W, sems = scratch[nparts:]
    n = a_ref.shape[0]
    nb = n // BLK
    np2 = n // 256
    r = place_ref[0]
    c = place_ref[1]

    early, late = [], []
    for i in range(nb):
        src = min(i, nb - 1 - i)
        first = 0 if 2 * i >= nb else BLK * (nb - i)
        for group, lo, hi in ((early, 0, min(2, i + 1)), (late, 2, i + 1)):
            if hi > lo:
                group.append(
                    pltpu.make_async_copy(
                        packed_ref.at[pl.ds(BLK * src, BLK), pl.ds(first + BLK * lo, BLK * (hi - lo))],
                        a_ref.at[pl.ds(BLK * i, BLK), pl.ds(BLK * lo, BLK * (hi - lo))],
                        sems.at[len(early) + len(late)],
                    )
                )
    for copy in early + late:
        copy.start()

    def zero(i, _):
        at = pl.ds(pl.multiple_of(i * 256, 256), 256)
        Q[at, :] = jnp.zeros((256, 256), jnp.float32)
        return 0

    lax.fori_loop(0, np2, zero, 0)
    out_ref[...] = jnp.zeros(out_ref.shape, jnp.float32)
    for copy in early:
        copy.wait()

    row_of = lax.broadcasted_iota(jnp.int32, (BLK, BLK), 0)
    col_of = lax.broadcasted_iota(jnp.int32, (BLK, BLK), 1)
    shift = jnp.where(row_of == col_of, SHIFT_NUM / 4.0, 0.0)

    def column(jj, _):
        J2 = jj // 2
        h = jj % 2
        base = pl.multiple_of(J2 * 256, 256)
        here = pl.multiple_of(jj * 128, 128)
        first = base // BT

        @pl.when(jj == 0)
        def _():
            def rows(i):
                at = pl.ds(i * BT, BT)
                P[at, :] = a_ref[at, :256]
            for i in range(n // BT):
                rows(i)

        @pl.when(jj == 1)
        def _():
            for copy in late:
                copy.wait()

        @pl.when((h == 0) & (jj > 0))
        def _():
            ks = pl.ds(pl.multiple_of(base - 256, 256), 256)
            def rows(i):
                at = pl.ds(i * BT, BT)
                P[at, :] = a_ref[at, pl.ds(base, 256)] + Q[at, :] - dot_nt([L[at, ks] for L in Ls], [L[pl.ds(base, 256), ks] for L in Ls])
                Q[at, :] = jnp.zeros((BT, 256), jnp.float32)
            each_tile(first, n, rows)

        @pl.when(h == 1)
        def _():
            prev = pl.ds(pl.multiple_of(here - 128, 128), 128)
            def rows(i):
                at = pl.ds(i * BT, BT)
                P[at, :128] = P[at, 128:] - dot_nt_narrow([L[at, prev] for L in Ls], [L[pl.ds(here, 128), prev] for L in Ls])
            each_tile(first, n, rows)

        units = (np2 // 2 * (np2 // 2 - 1) + 1) // 2
        later = jnp.minimum(J2 + 1, np2 - 1)
        deep = jnp.maximum(J2, 1)
        def unit(u):
            at = units * h + u
            real = at < J2 * (np2 - 1 - J2)
            i = J2 + 1 + at // deep
            src = pl.multiple_of(jnp.where(real, i, 0) * 256, 256)
            dst = pl.multiple_of(jnp.where(real, i, np2) * 256, 256)
            ks = pl.ds(pl.multiple_of(jnp.where(real, at % deep, 0) * 256, 256), 256)
            Q[pl.ds(dst, 256), :] -= dot_nt([L[pl.ds(src, 256), ks] for L in Ls], [L[pl.ds(pl.multiple_of(later * 256, 256), 256), ks] for L in Ls])
        def beside(t):
            if t % 2 == 0 and t // 2 < units:
                unit(t // 2)
        P[pl.ds(here, BLK), :BLK] += shift
        ws = diag128([P[pl.ds(pl.multiple_of(here + 8 * s, 8), 8), :128] for s in range(16)], beside)
        for s in range(16):
            W[8 * s:8 * s + 8, :] = ws[s]
        w = split(W[...], 3)
        def rows(i):
            at = pl.ds(i * BT, BT)
            l = dot_nt_narrow(split(P[at, :128], 3), w)
            for L, part in zip(Ls, split(l, nparts)):
                L[at, pl.ds(here, 128)] = part
            P[at, :128] = l
        each_tile(first, n, rows)

        @pl.when(jj == c)
        def _():
            rows = out_ref.shape[0]
            mine = P[pl.ds(pl.multiple_of(r * rows, rows), rows), :128]
            row = lax.broadcasted_iota(jnp.int32, mine.shape, 0) + r * rows
            col = lax.broadcasted_iota(jnp.int32, mine.shape, 1) + here
            out_ref[...] = jnp.where(row >= col, mine, 0.0)
        return 0
    lax.fori_loop(0, n // 128, column, 0)

    for q in range(2):
        i = 2 * r + q
        rows_i = pl.multiple_of(i * BLK, BLK)
        cols_c = pl.multiple_of(c * BLK, BLK)

        @pl.when(c <= i)
        def _():
            band_ref[q * BLK:(q + 1) * BLK, :] = a_ref[pl.ds(rows_i, BLK), pl.ds(cols_c, BLK)]

        @pl.when(c > i)
        def _():
            band_ref[q * BLK:(q + 1) * BLK, :] = a_ref[pl.ds(cols_c, BLK), pl.ds(rows_i, BLK)].T


def chol_piece(packed, place, n, rows, nparts=3):
    nb = n // BLK
    flat = jax.ShapeDtypeStruct((rows, BLK), jnp.float32)
    vmem = pl.BlockSpec(memory_space=pltpu.VMEM)
    return pl.pallas_call(
        functools.partial(chol_kernel, nparts),
        out_shape=(flat, flat),
        in_specs=[pl.BlockSpec(memory_space=pltpu.SMEM), pl.BlockSpec(memory_space=pl.ANY)],
        out_specs=(vmem, vmem),
        scratch_shapes=[pltpu.VMEM((n, n), jnp.float32)]
        + [pltpu.VMEM((n, n), jnp.bfloat16)] * nparts
        + [pltpu.VMEM((n, 256), jnp.float32), pltpu.VMEM((n + 256, 256), jnp.float32), pltpu.VMEM((BLK, BLK), jnp.float32), pltpu.SemaphoreType.DMA((2 * nb,))],
        compiler_params=pltpu.CompilerParams(vmem_limit_bytes=56 * 2**20),
        cost_estimate=pl.CostEstimate(flops=2 * n * n * n, bytes_accessed=300 * 2**20, transcendentals=n),
        name="factor",
    )(place, packed)


def band_kernel(keep_ref, slab_ref, band_ref, got, sems):
    ncols = band_ref.shape[1] // BLK
    step = slab_ref.shape[1] // ncols
    copies = [
        pltpu.make_async_copy(slab_ref.at[:, pl.ds(c * step, BLK)], got.at[:, pl.ds(c * BLK, BLK)], sems.at[c])
        for c in range(ncols)
    ]
    for copy in copies:
        copy.start()
    for c, copy in enumerate(copies):
        copy.wait()
        at = slice(c * BLK, (c + 1) * BLK)
        band_ref[:, at] = got[:, at] * keep_ref[0, c * step // BLK].astype(jnp.float32)


def band_columns(slab, block_mask, ncols):
    users = slab.shape[0]
    return pl.pallas_call(
        band_kernel,
        out_shape=jax.ShapeDtypeStruct((users, BLK * ncols), jnp.float32),
        in_specs=[pl.BlockSpec(memory_space=pltpu.SMEM), pl.BlockSpec(memory_space=pl.ANY)],
        out_specs=pl.BlockSpec(memory_space=pltpu.VMEM),
        scratch_shapes=[pltpu.VMEM((users, BLK * ncols), jnp.float32), pltpu.SemaphoreType.DMA((ncols,))],
        name="mask_band",
    )(block_mask, slab)


def rest_kernel(pair, keep_ref, slab_ref, rest_ref):
    g = pl.program_id(0)
    blocks = slab_ref.shape[1] // BLK
    per = blocks // pair
    to = 0
    for b in range(blocks):
        if b % per:
            keep = keep_ref[0, g * blocks + b].astype(jnp.float32)
            rest_ref[0, :, to:to + BLK] = slab_ref[:, b * BLK:(b + 1) * BLK] * keep
            to += BLK


def other_columns(slab, block_mask, ncols, nrows):
    users, items = slab.shape
    pair = ncols // nrows
    other = items // nrows - pair * BLK
    return pl.pallas_call(
        functools.partial(rest_kernel, pair),
        grid=(nrows,),
        out_shape=jax.ShapeDtypeStruct((nrows, users, other), jnp.float32),
        in_specs=[pl.BlockSpec(memory_space=pltpu.SMEM), pl.BlockSpec((users, items // nrows), lambda g: (0, g))],
        out_specs=pl.BlockSpec((1, users, other), lambda g: (g, 0, 0)),
        cost_estimate=pl.CostEstimate(flops=users * items, bytes_accessed=8 * users * items, transcendentals=0),
        name="mask_rest",
    )(block_mask, slab)


def shards(slab, block_mask):
    z, k, y, x = (lax.axis_index(axis) for axis in ("z", "k", "y", "x"))
    groups = lax.axis_size("y") * lax.axis_size("k")
    ncols = lax.axis_size("z") * lax.axis_size("x")
    g = lax.axis_size("k") * y + k
    pair = ncols // groups
    total_users = slab.shape[0] * ncols * groups
    high = dict(precision=lax.Precision.HIGH, preferred_element_type=jnp.float32)
    over_users = (((0,), (0,)), ((), ()))

    band = band_columns(slab, block_mask, ncols)
    rest = other_columns(slab, block_mask, ncols, groups)
    bands = lax.all_gather(band, ("y", "k"), axis=0, tiled=True)
    bands, rest = lax.optimization_barrier((bands, rest))

    upper = lax.dynamic_slice_in_dim(bands, BLK * g, BLK, 1)
    lower = lax.dynamic_slice_in_dim(bands, BLK * (ncols - 1 - g), BLK, 1)
    both = lax.dot_general(jnp.concatenate([lower, upper], axis=1), bands, over_users, **high)
    padded = jnp.concatenate([jnp.zeros((BLK, BLK * ncols), jnp.float32), both[BLK:]], axis=1)
    moved = lax.dynamic_slice_in_dim(padded, BLK * g, BLK * (ncols + 1), 1)
    long = jnp.concatenate([both[:BLK], jnp.zeros((BLK, BLK), jnp.float32)], axis=1)
    lane = lax.broadcasted_iota(jnp.int32, moved.shape, 1)
    packed = jnp.where(lane < BLK * (ncols - g), long, moved)
    pieces = lax.all_to_all(packed, ("z", "x"), split_axis=0, concat_axis=0, tiled=True)
    mine = jnp.sum(pieces.reshape(ncols, BLK // ncols, -1), axis=0) / total_users
    mine, rest = lax.optimization_barrier((mine, rest))
    panel = lax.all_gather(mine, ("y", "k", "z", "x"), axis=0, tiled=True)

    others = lax.all_to_all(rest, ("y", "k"), split_axis=0, concat_axis=0, tiled=True)
    others = others.reshape(-1, others.shape[-1])
    partial = lax.dot_general(bands, others, over_users, **high)
    parts = lax.all_to_all(partial, ("z", "x"), split_axis=0, concat_axis=0, tiled=True)

    place = jnp.stack([lax.axis_size("k") * z + k, lax.axis_size("x") * y + x]).astype(jnp.int32)
    block, piece = chol_piece(panel, place, BLK * ncols, BLK * pair)
    parts, block, piece = lax.optimization_barrier((parts, block, piece))
    strip = jnp.sum(parts.reshape(ncols, -1, parts.shape[1]), axis=0) / total_users
    half = strip.shape[1] // pair
    odd = x % 2
    own = lax.dynamic_slice_in_dim(strip, half * odd, half, 1)
    far = lax.dynamic_slice_in_dim(strip, half * (1 - odd), half, 1)
    nx = lax.axis_size("x")
    at = [(i, j) for i in range(lax.axis_size("k")) for j in range(nx)]
    to = lambda i, j: i * nx + j
    own = lax.ppermute(own, ("k", "x"), [(to(i, j), to(j // 2, 2 * i + j % 2)) for i, j in at])
    far = lax.ppermute(far, ("k", "x"), [(to(i, j), to(j // 2, 2 * i + 1 - j % 2)) for i, j in at])
    items = jnp.where(odd == 0, jnp.concatenate([own, far]), jnp.concatenate([far, own]))
    return (jnp.concatenate([block, items], axis=1), piece)


def solution(mesh):
    rows, cols = mesh.devices.shape
    axes = ("z", "k", "y", "x")
    fine = Mesh(mesh.devices.reshape(rows // 2, 2, cols // 4, 4), axes)
    return jax.shard_map(
        shards,
        mesh=fine,
        in_specs=(P(axes, None), P(axes, None)),
        out_specs=(P(("z", "k"), ("y", "x")), P(("z", "k"), ("y", "x"))),
        check_vma=False,
    )
```

```python
import functools

import jax
import jax.numpy as jnp
from jax import lax
from jax.experimental import pallas as pl
from jax.experimental.pallas import tpu as pltpu
from jax.sharding import Mesh
from jax.sharding import PartitionSpec as P

BLK = 128
SHIFT_NUM = 2


def diag128(F, beside=lambda t: None):
    S = (8, 128)
    lane = lax.broadcasted_iota(jnp.int32, S, 1)
    subl = lax.broadcasted_iota(jnp.int32, S, 0)
    F = list(F)
    Ws = []
    onehot = [jnp.where(subl == k, 1.0, 0.0) for k in range(8)]
    n = len(F)
    spread = lambda x, at: [jnp.broadcast_to(x[:, at + k:at + k + 1], S) for k in range(8)]
    D = spread(F[0], 0)
    for t in range(n):
        b = 8 * t
        inblk = (lane >= b) & (lane < b + 8)
        X = jnp.where(inblk, jnp.where(lane - b == subl, 1.0, 0.0), F[t])
        if t + 1 < n:
            first = spread(F[t + 1], b)
            B = list(first)
            N = spread(F[t + 1], b + 8)
        C = {}
        for k in range(8):
            for s in range(t + 2, n):
                C[s, k] = jnp.broadcast_to(F[s][:, b + k:b + k + 1], S)
        G = jnp.zeros(S, jnp.float32)
        for k in range(8):
            d = jnp.broadcast_to(D[k][k:k + 1], S)
            rs = lax.rsqrt(d)
            inv = 1.0 / d
            g = D[k] - onehot[k]
            xk = jnp.broadcast_to(X[k:k + 1], S)
            G = jnp.where(subl == k, xk * rs, G)
            X = X - g * (xk * inv)
            for m in range(k + 1, 8):
                f = jnp.broadcast_to(D[m][k:k + 1], S) * inv
                D[m] = D[m] - g * f
                if t + 1 < n:
                    B[m] = B[m] - B[k] * f
            if t + 1 < n:
                y = B[k] * inv
                N = [N[m] - B[k] * jnp.broadcast_to(y[m:m + 1], S) for m in range(8)]
        Ws.append(jnp.where(lane < b + 8, G, 0.0))
        if t + 1 < n:
            V = [jnp.broadcast_to(X[k:k + 1], S) for k in range(8)]
            for s in range(t + 1, n):
                f = jnp.where(inblk, 0.0, F[s])
                for k in range(8):
                    f = f - (first[k] if s == t + 1 else C[s, k]) * V[k]
                F[s] = f
            D = N
        beside(t)
    return Ws


def split(x, n):
    parts = []
    for i in range(n):
        h = x.astype(jnp.bfloat16)
        parts.append(h)
        if i + 1 < n:
            x = x - h.astype(jnp.float32)
    return parts

PAIRS = {2: [(0, 0), (0, 1), (1, 0)], 3: [(0, 0), (0, 1), (1, 0), (0, 2), (1, 1), (2, 0)]}

def dot_nt(a, b):
    pairs = PAIRS[len(a)]
    x = jnp.concatenate([a[i] for i, _ in pairs], axis=1)
    y = jnp.concatenate([b[j] for _, j in pairs], axis=1)
    return lax.dot_general(x, y, (((1,), (1,)), ((), ())), preferred_element_type=jnp.float32)

def dot_nt_narrow(a, b):
    rows = b[0].shape[0]
    x = jnp.concatenate([a[0], a[1]], axis=1)
    y = jnp.concatenate([jnp.concatenate([b[0], b[1]], axis=1), jnp.concatenate([b[1], b[0]], axis=1)], axis=0)
    u = lax.dot_general(x, y, (((1,), (1,)), ((), ())), preferred_element_type=jnp.float32)
    x = jnp.concatenate([a[0], a[2]], axis=1)
    y = jnp.concatenate([b[2], b[0]], axis=1)
    v = lax.dot_general(x, y, (((1,), (1,)), ((), ())), preferred_element_type=jnp.float32)
    return u[:, :rows] + (u[:, rows:] + v)


BT = 256


def each_tile(first, n, body):
    for f in range(n // BT):

        @pl.when(first == f)
        def _():
            for i in range(f, n // BT):
                body(i)


def chol_kernel(nparts, place_ref, packed_ref, band_ref, out_ref, a_ref, *scratch):
    Ls = scratch[:nparts]
    P, Q, W, sems = scratch[nparts:]
    n = a_ref.shape[0]
    nb = n // BLK
    np2 = n // 256
    r = place_ref[0]
    c = place_ref[1]

    early, late = [], []
    for i in range(nb):
        src = min(i, nb - 1 - i)
        first = 0 if 2 * i >= nb else BLK * (nb - i)
        for group, lo, hi in ((early, 0, min(2, i + 1)), (late, 2, i + 1)):
            if hi > lo:
                group.append(
                    pltpu.make_async_copy(
                        packed_ref.at[pl.ds(BLK * src, BLK), pl.ds(first + BLK * lo, BLK * (hi - lo))],
                        a_ref.at[pl.ds(BLK * i, BLK), pl.ds(BLK * lo, BLK * (hi - lo))],
                        sems.at[len(early) + len(late)],
                    )
                )
    for copy in early + late:
        copy.start()

    def zero(i, _):
        at = pl.ds(pl.multiple_of(i * 256, 256), 256)
        Q[at, :] = jnp.zeros((256, 256), jnp.float32)
        return 0

    lax.fori_loop(0, np2, zero, 0)
    out_ref[...] = jnp.zeros(out_ref.shape, jnp.float32)
    for copy in early:
        copy.wait()

    row_of = lax.broadcasted_iota(jnp.int32, (BLK, BLK), 0)
    col_of = lax.broadcasted_iota(jnp.int32, (BLK, BLK), 1)
    shift = jnp.where(row_of == col_of, SHIFT_NUM / 4.0, 0.0)

    def column(jj, _):
        J2 = jj // 2
        h = jj % 2
        base = pl.multiple_of(J2 * 256, 256)
        here = pl.multiple_of(jj * 128, 128)
        first = base // BT

        @pl.when(jj == 0)
        def _():
            def rows(i):
                at = pl.ds(i * BT, BT)
                P[at, :] = a_ref[at, :256]
            for i in range(n // BT):
                rows(i)

        @pl.when(jj == 1)
        def _():
            for copy in late:
                copy.wait()

        @pl.when((h == 0) & (jj > 0))
        def _():
            ks = pl.ds(pl.multiple_of(base - 256, 256), 256)
            def rows(i):
                at = pl.ds(i * BT, BT)
                P[at, :] = a_ref[at, pl.ds(base, 256)] + Q[at, :] - dot_nt([L[at, ks] for L in Ls], [L[pl.ds(base, 256), ks] for L in Ls])
                Q[at, :] = jnp.zeros((BT, 256), jnp.float32)
            each_tile(first, n, rows)

        @pl.when(h == 1)
        def _():
            prev = pl.ds(pl.multiple_of(here - 128, 128), 128)
            def rows(i):
                at = pl.ds(i * BT, BT)
                P[at, :128] = P[at, 128:] - dot_nt_narrow([L[at, prev] for L in Ls], [L[pl.ds(here, 128), prev] for L in Ls])
            each_tile(first, n, rows)

        units = (np2 // 2 * (np2 // 2 - 1) + 1) // 2
        later = jnp.minimum(J2 + 1, np2 - 1)
        deep = jnp.maximum(J2, 1)
        def unit(u):
            at = units * h + u
            real = at < J2 * (np2 - 1 - J2)
            i = J2 + 1 + at // deep
            src = pl.multiple_of(jnp.where(real, i, 0) * 256, 256)
            dst = pl.multiple_of(jnp.where(real, i, np2) * 256, 256)
            ks = pl.ds(pl.multiple_of(jnp.where(real, at % deep, 0) * 256, 256), 256)
            Q[pl.ds(dst, 256), :] -= dot_nt([L[pl.ds(src, 256), ks] for L in Ls], [L[pl.ds(pl.multiple_of(later * 256, 256), 256), ks] for L in Ls])
        def beside(t):
            if t % 2 == 0 and t // 2 < units:
                unit(t // 2)
        P[pl.ds(here, BLK), :BLK] += shift
        ws = diag128([P[pl.ds(pl.multiple_of(here + 8 * s, 8), 8), :128] for s in range(16)], beside)
        for s in range(16):
            W[8 * s:8 * s + 8, :] = ws[s]
        w = split(W[...], 3)
        def rows(i):
            at = pl.ds(i * BT, BT)
            l = dot_nt_narrow(split(P[at, :128], 3), w)
            for L, part in zip(Ls, split(l, nparts)):
                L[at, pl.ds(here, 128)] = part
            P[at, :128] = l
        each_tile(first, n, rows)

        @pl.when(jj == c)
        def _():
            rows = out_ref.shape[0]
            mine = P[pl.ds(pl.multiple_of(r * rows, rows), rows), :128]
            row = lax.broadcasted_iota(jnp.int32, mine.shape, 0) + r * rows
            col = lax.broadcasted_iota(jnp.int32, mine.shape, 1) + here
            out_ref[...] = jnp.where(row >= col, mine, 0.0)
        return 0
    lax.fori_loop(0, n // 128, column, 0)

    for q in range(2):
        i = 2 * r + q
        rows_i = pl.multiple_of(i * BLK, BLK)
        cols_c = pl.multiple_of(c * BLK, BLK)

        @pl.when(c <= i)
        def _():
            band_ref[q * BLK:(q + 1) * BLK, :] = a_ref[pl.ds(rows_i, BLK), pl.ds(cols_c, BLK)]

        @pl.when(c > i)
        def _():
            band_ref[q * BLK:(q + 1) * BLK, :] = a_ref[pl.ds(cols_c, BLK), pl.ds(rows_i, BLK)].T


def chol_piece(packed, place, n, rows, nparts=3):
    nb = n // BLK
    flat = jax.ShapeDtypeStruct((rows, BLK), jnp.float32)
    vmem = pl.BlockSpec(memory_space=pltpu.VMEM)
    return pl.pallas_call(
        functools.partial(chol_kernel, nparts),
        out_shape=(flat, flat),
        in_specs=[pl.BlockSpec(memory_space=pltpu.SMEM), pl.BlockSpec(memory_space=pl.ANY)],
        out_specs=(vmem, vmem),
        scratch_shapes=[pltpu.VMEM((n, n), jnp.float32)]
        + [pltpu.VMEM((n, n), jnp.bfloat16)] * nparts
        + [pltpu.VMEM((n, 256), jnp.float32), pltpu.VMEM((n + 256, 256), jnp.float32), pltpu.VMEM((BLK, BLK), jnp.float32), pltpu.SemaphoreType.DMA((2 * nb,))],
        compiler_params=pltpu.CompilerParams(vmem_limit_bytes=56 * 2**20),
        cost_estimate=pl.CostEstimate(flops=2 * n * n * n, bytes_accessed=300 * 2**20, transcendentals=n),
        name="factor",
    )(place, packed)


def band_kernel(keep_ref, slab_ref, band_ref, got, sems):
    ncols = band_ref.shape[1] // BLK
    step = slab_ref.shape[1] // ncols
    copies = [
        pltpu.make_async_copy(slab_ref.at[:, pl.ds(c * step, BLK)], got.at[:, pl.ds(c * BLK, BLK)], sems.at[c])
        for c in range(ncols)
    ]
    for copy in copies:
        copy.start()
    for c, copy in enumerate(copies):
        copy.wait()
        at = slice(c * BLK, (c + 1) * BLK)
        band_ref[:, at] = got[:, at] * keep_ref[0, c * step // BLK].astype(jnp.float32)


def band_columns(slab, block_mask, ncols):
    users = slab.shape[0]
    return pl.pallas_call(
        band_kernel,
        out_shape=jax.ShapeDtypeStruct((users, BLK * ncols), jnp.float32),
        in_specs=[pl.BlockSpec(memory_space=pltpu.SMEM), pl.BlockSpec(memory_space=pl.ANY)],
        out_specs=pl.BlockSpec(memory_space=pltpu.VMEM),
        scratch_shapes=[pltpu.VMEM((users, BLK * ncols), jnp.float32), pltpu.SemaphoreType.DMA((ncols,))],
        name="mask_band",
    )(block_mask, slab)


def rest_kernel(pair, keep_ref, slab_ref, rest_ref):
    g = pl.program_id(0)
    blocks = slab_ref.shape[1] // BLK
    per = blocks // pair
    to = 0
    for b in range(blocks):
        if b % per:
            keep = keep_ref[0, g * blocks + b].astype(jnp.float32)
            rest_ref[0, :, to:to + BLK] = slab_ref[:, b * BLK:(b + 1) * BLK] * keep
            to += BLK


def other_columns(slab, block_mask, ncols, nrows):
    users, items = slab.shape
    pair = ncols // nrows
    other = items // nrows - pair * BLK
    return pl.pallas_call(
        functools.partial(rest_kernel, pair),
        grid=(nrows,),
        out_shape=jax.ShapeDtypeStruct((nrows, users, other), jnp.float32),
        in_specs=[pl.BlockSpec(memory_space=pltpu.SMEM), pl.BlockSpec((users, items // nrows), lambda g: (0, g))],
        out_specs=pl.BlockSpec((1, users, other), lambda g: (g, 0, 0)),
        cost_estimate=pl.CostEstimate(flops=users * items, bytes_accessed=8 * users * items, transcendentals=0),
        name="mask_rest",
    )(block_mask, slab)


def shards(slab, block_mask):
    z, k, y, x = (lax.axis_index(axis) for axis in ("z", "k", "y", "x"))
    groups = lax.axis_size("y") * lax.axis_size("k")
    ncols = lax.axis_size("z") * lax.axis_size("x")
    g = lax.axis_size("k") * y + k
    pair = ncols // groups
    total_users = slab.shape[0] * ncols * groups
    high = dict(precision=lax.Precision.HIGH, preferred_element_type=jnp.float32)
    over_users = (((0,), (0,)), ((), ()))

    band = band_columns(slab, block_mask, ncols)
    rest = other_columns(slab, block_mask, ncols, groups)
    bands = lax.all_gather(band, ("y", "k"), axis=0, tiled=True)
    bands, rest = lax.optimization_barrier((bands, rest))

    upper = lax.dynamic_slice_in_dim(bands, BLK * g, BLK, 1)
    lower = lax.dynamic_slice_in_dim(bands, BLK * (ncols - 1 - g), BLK, 1)
    both = lax.dot_general(jnp.concatenate([lower, upper], axis=1), bands, over_users, **high)
    padded = jnp.concatenate([jnp.zeros((BLK, BLK * ncols), jnp.float32), both[BLK:]], axis=1)
    moved = lax.dynamic_slice_in_dim(padded, BLK * g, BLK * (ncols + 1), 1)
    long = jnp.concatenate([both[:BLK], jnp.zeros((BLK, BLK), jnp.float32)], axis=1)
    lane = lax.broadcasted_iota(jnp.int32, moved.shape, 1)
    packed = jnp.where(lane < BLK * (ncols - g), long, moved)
    pieces = lax.all_to_all(packed, ("z", "x"), split_axis=0, concat_axis=0, tiled=True)
    mine = jnp.sum(pieces.reshape(ncols, BLK // ncols, -1), axis=0) / total_users
    mine, rest = lax.optimization_barrier((mine, rest))
    panel = lax.all_gather(mine, ("y", "k", "z", "x"), axis=0, tiled=True)

    others = lax.all_to_all(rest, ("y", "k"), split_axis=0, concat_axis=0, tiled=True)
    others = others.reshape(-1, others.shape[-1])
    partial = lax.dot_general(bands, others, over_users, **high)
    panel, partial = lax.optimization_barrier((panel, partial))
    strip = lax.psum_scatter(partial, ("z", "x"), scatter_dimension=0, tiled=True)

    place = jnp.stack([lax.axis_size("k") * z + k, lax.axis_size("x") * y + x]).astype(jnp.int32)
    block, piece = chol_piece(panel, place, BLK * ncols, BLK * pair)
    strip, block, piece = lax.optimization_barrier((strip, block, piece))
    half = strip.shape[1] // pair
    odd = x % 2
    own = lax.dynamic_slice_in_dim(strip, half * odd, half, 1)
    far = lax.dynamic_slice_in_dim(strip, half * (1 - odd), half, 1)
    nx = lax.axis_size("x")
    at = [(i, j) for i in range(lax.axis_size("k")) for j in range(nx)]
    to = lambda i, j: i * nx + j
    own = lax.ppermute(own, ("k", "x"), [(to(i, j), to(j // 2, 2 * i + j % 2)) for i, j in at])
    far = lax.ppermute(far, ("k", "x"), [(to(i, j), to(j // 2, 2 * i + 1 - j % 2)) for i, j in at])
    items = jnp.where(odd == 0, jnp.concatenate([own, far]), jnp.concatenate([far, own])) / total_users
    return (jnp.concatenate([block, items], axis=1), piece)


def solution(mesh):
    rows, cols = mesh.devices.shape
    axes = ("z", "k", "y", "x")
    fine = Mesh(mesh.devices.reshape(rows // 2, 2, cols // 4, 4), axes)
    return jax.shard_map(
        shards,
        mesh=fine,
        in_specs=(P(axes, None), P(axes, None)),
        out_specs=(P(("z", "k"), ("y", "x")), P(("z", "k"), ("y", "x"))),
        check_vma=False,
    )
```

```python
import functools

import jax
import jax.numpy as jnp
from jax import lax
from jax.experimental import pallas as pl
from jax.experimental.pallas import tpu as pltpu
from jax.sharding import Mesh
from jax.sharding import PartitionSpec as P

BLK = 128
SHIFT_NUM = 2


def diag128(F, beside=lambda t: None):
    S = (8, 128)
    lane = lax.broadcasted_iota(jnp.int32, S, 1)
    subl = lax.broadcasted_iota(jnp.int32, S, 0)
    F = list(F)
    Ws = []
    onehot = [jnp.where(subl == k, 1.0, 0.0) for k in range(8)]
    n = len(F)
    spread = lambda x, at: [jnp.broadcast_to(x[:, at + k:at + k + 1], S) for k in range(8)]
    D = spread(F[0], 0)
    for t in range(n):
        b = 8 * t
        inblk = (lane >= b) & (lane < b + 8)
        X = jnp.where(inblk, jnp.where(lane - b == subl, 1.0, 0.0), F[t])
        if t + 1 < n:
            first = spread(F[t + 1], b)
            B = list(first)
            N = spread(F[t + 1], b + 8)
        C = {}
        for k in range(8):
            for s in range(t + 2, n):
                C[s, k] = jnp.broadcast_to(F[s][:, b + k:b + k + 1], S)
        G = jnp.zeros(S, jnp.float32)
        for k in range(8):
            d = jnp.broadcast_to(D[k][k:k + 1], S)
            rs = lax.rsqrt(d)
            inv = 1.0 / d
            g = D[k] - onehot[k]
            xk = jnp.broadcast_to(X[k:k + 1], S)
            G = jnp.where(subl == k, xk * rs, G)
            X = X - g * (xk * inv)
            for m in range(k + 1, 8):
                f = jnp.broadcast_to(D[m][k:k + 1], S) * inv
                D[m] = D[m] - g * f
                if t + 1 < n:
                    B[m] = B[m] - B[k] * f
            if t + 1 < n:
                y = B[k] * inv
                N = [N[m] - B[k] * jnp.broadcast_to(y[m:m + 1], S) for m in range(8)]
        Ws.append(jnp.where(lane < b + 8, G, 0.0))
        if t + 1 < n:
            V = [jnp.broadcast_to(X[k:k + 1], S) for k in range(8)]
            for s in range(t + 1, n):
                f = jnp.where(inblk, 0.0, F[s])
                for k in range(8):
                    f = f - (first[k] if s == t + 1 else C[s, k]) * V[k]
                F[s] = f
            D = N
        beside(t)
    return Ws


def split(x, n):
    parts = []
    for i in range(n):
        h = x.astype(jnp.bfloat16)
        parts.append(h)
        if i + 1 < n:
            x = x - h.astype(jnp.float32)
    return parts

PAIRS = {2: [(0, 0), (0, 1), (1, 0)], 3: [(0, 0), (0, 1), (1, 0), (0, 2), (1, 1), (2, 0)]}

def dot_nt(a, b):
    pairs = PAIRS[len(a)]
    x = jnp.concatenate([a[i] for i, _ in pairs], axis=1)
    y = jnp.concatenate([b[j] for _, j in pairs], axis=1)
    return lax.dot_general(x, y, (((1,), (1,)), ((), ())), preferred_element_type=jnp.float32)

def dot_nt_narrow(a, b):
    rows = b[0].shape[0]
    x = jnp.concatenate([a[0], a[1]], axis=1)
    y = jnp.concatenate([jnp.concatenate([b[0], b[1]], axis=1), jnp.concatenate([b[1], b[0]], axis=1)], axis=0)
    u = lax.dot_general(x, y, (((1,), (1,)), ((), ())), preferred_element_type=jnp.float32)
    x = jnp.concatenate([a[0], a[2]], axis=1)
    y = jnp.concatenate([b[2], b[0]], axis=1)
    v = lax.dot_general(x, y, (((1,), (1,)), ((), ())), preferred_element_type=jnp.float32)
    return u[:, :rows] + (u[:, rows:] + v)


BT = 256


def each_tile(first, n, body):
    for f in range(n // BT):

        @pl.when(first == f)
        def _():
            for i in range(f, n // BT):
                body(i)


def chol_kernel(nparts, place_ref, packed_ref, band_ref, out_ref, a_ref, *scratch):
    Ls = scratch[:nparts]
    P, Q, W, sems = scratch[nparts:]
    n = a_ref.shape[0]
    nb = n // BLK
    np2 = n // 256
    r = place_ref[0]
    c = place_ref[1]

    early, late = [], []
    for i in range(nb):
        src = min(i, nb - 1 - i)
        first = 0 if 2 * i >= nb else BLK * (nb - i)
        for group, lo, hi in ((early, 0, min(2, i + 1)), (late, 2, i + 1)):
            if hi > lo:
                group.append(
                    pltpu.make_async_copy(
                        packed_ref.at[pl.ds(BLK * src, BLK), pl.ds(first + BLK * lo, BLK * (hi - lo))],
                        a_ref.at[pl.ds(BLK * i, BLK), pl.ds(BLK * lo, BLK * (hi - lo))],
                        sems.at[len(early) + len(late)],
                    )
                )
    for copy in early + late:
        copy.start()

    def zero(i, _):
        at = pl.ds(pl.multiple_of(i * 256, 256), 256)
        Q[at, :] = jnp.zeros((256, 256), jnp.float32)
        return 0

    lax.fori_loop(0, np2, zero, 0)
    out_ref[...] = jnp.zeros(out_ref.shape, jnp.float32)
    for copy in early:
        copy.wait()

    row_of = lax.broadcasted_iota(jnp.int32, (BLK, BLK), 0)
    col_of = lax.broadcasted_iota(jnp.int32, (BLK, BLK), 1)
    shift = jnp.where(row_of == col_of, SHIFT_NUM / 4.0, 0.0)

    def column(jj, _):
        J2 = jj // 2
        h = jj % 2
        base = pl.multiple_of(J2 * 256, 256)
        here = pl.multiple_of(jj * 128, 128)
        first = base // BT

        @pl.when(jj == 0)
        def _():
            def rows(i):
                at = pl.ds(i * BT, BT)
                P[at, :] = a_ref[at, :256]
            for i in range(n // BT):
                rows(i)

        @pl.when(jj == 1)
        def _():
            for copy in late:
                copy.wait()

        @pl.when((h == 0) & (jj > 0))
        def _():
            ks = pl.ds(pl.multiple_of(base - 256, 256), 256)
            def rows(i):
                at = pl.ds(i * BT, BT)
                P[at, :] = a_ref[at, pl.ds(base, 256)] + Q[at, :] - dot_nt([L[at, ks] for L in Ls], [L[pl.ds(base, 256), ks] for L in Ls])
                Q[at, :] = jnp.zeros((BT, 256), jnp.float32)
            each_tile(first, n, rows)

        @pl.when(h == 1)
        def _():
            prev = pl.ds(pl.multiple_of(here - 128, 128), 128)
            def rows(i):
                at = pl.ds(i * BT, BT)
                P[at, :128] = P[at, 128:] - dot_nt_narrow([L[at, prev] for L in Ls], [L[pl.ds(here, 128), prev] for L in Ls])
            each_tile(first, n, rows)

        units = (np2 // 2 * (np2 // 2 - 1) + 1) // 2
        later = jnp.minimum(J2 + 1, np2 - 1)
        deep = jnp.maximum(J2, 1)
        def unit(u):
            at = units * h + u
            real = at < J2 * (np2 - 1 - J2)
            i = J2 + 1 + at // deep
            src = pl.multiple_of(jnp.where(real, i, 0) * 256, 256)
            dst = pl.multiple_of(jnp.where(real, i, np2) * 256, 256)
            ks = pl.ds(pl.multiple_of(jnp.where(real, at % deep, 0) * 256, 256), 256)
            Q[pl.ds(dst, 256), :] -= dot_nt([L[pl.ds(src, 256), ks] for L in Ls], [L[pl.ds(pl.multiple_of(later * 256, 256), 256), ks] for L in Ls])
        def beside(t):
            if t % 2 == 0 and t // 2 < units:
                unit(t // 2)
        P[pl.ds(here, BLK), :BLK] += shift
        ws = diag128([P[pl.ds(pl.multiple_of(here + 8 * s, 8), 8), :128] for s in range(16)], beside)
        for s in range(16):
            W[8 * s:8 * s + 8, :] = ws[s]
        w = split(W[...], 3)
        def rows(i):
            at = pl.ds(i * BT, BT)
            l = dot_nt_narrow(split(P[at, :128], 3), w)
            for L, part in zip(Ls, split(l, nparts)):
                L[at, pl.ds(here, 128)] = part
            P[at, :128] = l
        each_tile(first, n, rows)

        @pl.when(jj == c)
        def _():
            rows = out_ref.shape[0]
            mine = P[pl.ds(pl.multiple_of(r * rows, rows), rows), :128]
            row = lax.broadcasted_iota(jnp.int32, mine.shape, 0) + r * rows
            col = lax.broadcasted_iota(jnp.int32, mine.shape, 1) + here
            out_ref[...] = jnp.where(row >= col, mine, 0.0)
        return 0
    lax.fori_loop(0, n // 128, column, 0)

    for q in range(2):
        i = 2 * r + q
        rows_i = pl.multiple_of(i * BLK, BLK)
        cols_c = pl.multiple_of(c * BLK, BLK)

        @pl.when(c <= i)
        def _():
            band_ref[q * BLK:(q + 1) * BLK, :] = a_ref[pl.ds(rows_i, BLK), pl.ds(cols_c, BLK)]

        @pl.when(c > i)
        def _():
            band_ref[q * BLK:(q + 1) * BLK, :] = a_ref[pl.ds(cols_c, BLK), pl.ds(rows_i, BLK)].T


def chol_piece(packed, place, n, rows, nparts=3):
    nb = n // BLK
    flat = jax.ShapeDtypeStruct((rows, BLK), jnp.float32)
    vmem = pl.BlockSpec(memory_space=pltpu.VMEM)
    return pl.pallas_call(
        functools.partial(chol_kernel, nparts),
        out_shape=(flat, flat),
        in_specs=[pl.BlockSpec(memory_space=pltpu.SMEM), pl.BlockSpec(memory_space=pl.ANY)],
        out_specs=(vmem, vmem),
        scratch_shapes=[pltpu.VMEM((n, n), jnp.float32)]
        + [pltpu.VMEM((n, n), jnp.bfloat16)] * nparts
        + [pltpu.VMEM((n, 256), jnp.float32), pltpu.VMEM((n + 256, 256), jnp.float32), pltpu.VMEM((BLK, BLK), jnp.float32), pltpu.SemaphoreType.DMA((2 * nb,))],
        compiler_params=pltpu.CompilerParams(vmem_limit_bytes=56 * 2**20),
        cost_estimate=pl.CostEstimate(flops=2 * n * n * n, bytes_accessed=300 * 2**20, transcendentals=n),
        name="factor",
    )(place, packed)


def band_kernel(scale, keep_ref, slab_ref, band_ref, got, sems):
    ncols = band_ref.shape[1] // BLK
    step = slab_ref.shape[1] // ncols
    copies = [
        pltpu.make_async_copy(slab_ref.at[:, pl.ds(c * step, BLK)], got.at[:, pl.ds(c * BLK, BLK)], sems.at[c])
        for c in range(ncols)
    ]
    for copy in copies:
        copy.start()
    for c, copy in enumerate(copies):
        copy.wait()
        at = slice(c * BLK, (c + 1) * BLK)
        band_ref[:, at] = got[:, at] * (keep_ref[0, c * step // BLK].astype(jnp.float32) * scale)


def band_columns(slab, block_mask, ncols, scale):
    users = slab.shape[0]
    return pl.pallas_call(
        functools.partial(band_kernel, scale),
        out_shape=jax.ShapeDtypeStruct((users, BLK * ncols), jnp.float32),
        in_specs=[pl.BlockSpec(memory_space=pltpu.SMEM), pl.BlockSpec(memory_space=pl.ANY)],
        out_specs=pl.BlockSpec(memory_space=pltpu.VMEM),
        scratch_shapes=[pltpu.VMEM((users, BLK * ncols), jnp.float32), pltpu.SemaphoreType.DMA((ncols,))],
        name="mask_band",
    )(block_mask, slab)


def rest_kernel(pair, scale, keep_ref, slab_ref, rest_ref):
    g = pl.program_id(0)
    blocks = slab_ref.shape[1] // BLK
    per = blocks // pair
    to = 0
    for b in range(blocks):
        if b % per:
            keep = keep_ref[0, g * blocks + b].astype(jnp.float32) * scale
            rest_ref[0, :, to:to + BLK] = slab_ref[:, b * BLK:(b + 1) * BLK] * keep
            to += BLK


def other_columns(slab, block_mask, ncols, nrows, scale):
    users, items = slab.shape
    pair = ncols // nrows
    other = items // nrows - pair * BLK
    return pl.pallas_call(
        functools.partial(rest_kernel, pair, scale),
        grid=(nrows,),
        out_shape=jax.ShapeDtypeStruct((nrows, users, other), jnp.float32),
        in_specs=[pl.BlockSpec(memory_space=pltpu.SMEM), pl.BlockSpec((users, items // nrows), lambda g: (0, g))],
        out_specs=pl.BlockSpec((1, users, other), lambda g: (g, 0, 0)),
        cost_estimate=pl.CostEstimate(flops=users * items, bytes_accessed=8 * users * items, transcendentals=0),
        name="mask_rest",
    )(block_mask, slab)


def shards(slab, block_mask):
    z, k, y, x = (lax.axis_index(axis) for axis in ("z", "k", "y", "x"))
    groups = lax.axis_size("y") * lax.axis_size("k")
    ncols = lax.axis_size("z") * lax.axis_size("x")
    g = lax.axis_size("k") * y + k
    pair = ncols // groups
    total_users = slab.shape[0] * ncols * groups
    high = dict(precision=lax.Precision.HIGH, preferred_element_type=jnp.float32)
    over_users = (((0,), (0,)), ((), ()))

    scale = 2.0 ** -(total_users.bit_length() // 2)
    assert scale * scale * total_users == 1.0
    band = band_columns(slab, block_mask, ncols, scale)
    rest = other_columns(slab, block_mask, ncols, groups, scale)
    bands = lax.all_gather(band, ("y", "k"), axis=0, tiled=True)
    bands, rest = lax.optimization_barrier((bands, rest))

    upper = lax.dynamic_slice_in_dim(bands, BLK * g, BLK, 1)
    lower = lax.dynamic_slice_in_dim(bands, BLK * (ncols - 1 - g), BLK, 1)
    both = lax.dot_general(jnp.concatenate([lower, upper], axis=1), bands, over_users, **high)
    padded = jnp.concatenate([jnp.zeros((BLK, BLK * ncols), jnp.float32), both[BLK:]], axis=1)
    moved = lax.dynamic_slice_in_dim(padded, BLK * g, BLK * (ncols + 1), 1)
    long = jnp.concatenate([both[:BLK], jnp.zeros((BLK, BLK), jnp.float32)], axis=1)
    lane = lax.broadcasted_iota(jnp.int32, moved.shape, 1)
    packed = jnp.where(lane < BLK * (ncols - g), long, moved)
    pieces = lax.all_to_all(packed, ("z", "x"), split_axis=0, concat_axis=0, tiled=True)
    mine = jnp.sum(pieces.reshape(ncols, BLK // ncols, -1), axis=0)
    mine, rest = lax.optimization_barrier((mine, rest))
    panel = lax.all_gather(mine, ("y", "k", "z", "x"), axis=0, tiled=True)

    others = lax.all_to_all(rest, ("y", "k"), split_axis=0, concat_axis=0, tiled=True)
    others = others.reshape(-1, others.shape[-1])
    partial = lax.dot_general(bands, others, over_users, **high)
    strip = lax.psum_scatter(partial, ("z", "x"), scatter_dimension=0, tiled=True)

    place = jnp.stack([lax.axis_size("k") * z + k, lax.axis_size("x") * y + x]).astype(jnp.int32)
    block, piece = chol_piece(panel, place, BLK * ncols, BLK * pair)
    strip, block, piece = lax.optimization_barrier((strip, block, piece))
    half = strip.shape[1] // pair
    odd = x % 2
    own = lax.dynamic_slice_in_dim(strip, half * odd, half, 1)
    far = lax.dynamic_slice_in_dim(strip, half * (1 - odd), half, 1)
    nx = lax.axis_size("x")
    at = [(i, j) for i in range(lax.axis_size("k")) for j in range(nx)]
    to = lambda i, j: i * nx + j
    own = lax.ppermute(own, ("k", "x"), [(to(i, j), to(j // 2, 2 * i + j % 2)) for i, j in at])
    far = lax.ppermute(far, ("k", "x"), [(to(i, j), to(j // 2, 2 * i + 1 - j % 2)) for i, j in at])
    items = jnp.where(odd == 0, jnp.concatenate([own, far]), jnp.concatenate([far, own]))
    return (jnp.concatenate([block, items], axis=1), piece)


def solution(mesh):
    rows, cols = mesh.devices.shape
    axes = ("z", "k", "y", "x")
    fine = Mesh(mesh.devices.reshape(rows // 2, 2, cols // 4, 4), axes)
    return jax.shard_map(
        shards,
        mesh=fine,
        in_specs=(P(axes, None), P(axes, None)),
        out_specs=(P(("z", "k"), ("y", "x")), P(("z", "k"), ("y", "x"))),
        check_vma=False,
    )
```

```python
import functools

import jax
import jax.numpy as jnp
from jax import lax
from jax.experimental import pallas as pl
from jax.experimental.pallas import tpu as pltpu
from jax.sharding import Mesh
from jax.sharding import PartitionSpec as P

BLK = 128
SHIFT_NUM = 2


def diag128(F, beside=lambda t: None):
    S = (8, 128)
    lane = lax.broadcasted_iota(jnp.int32, S, 1)
    subl = lax.broadcasted_iota(jnp.int32, S, 0)
    F = list(F)
    Ws = []
    onehot = [jnp.where(subl == k, 1.0, 0.0) for k in range(8)]
    n = len(F)
    spread = lambda x, at: [jnp.broadcast_to(x[:, at + k:at + k + 1], S) for k in range(8)]
    D = spread(F[0], 0)
    for t in range(n):
        b = 8 * t
        inblk = (lane >= b) & (lane < b + 8)
        X = jnp.where(inblk, jnp.where(lane - b == subl, 1.0, 0.0), F[t])
        if t + 1 < n:
            first = spread(F[t + 1], b)
            B = list(first)
            N = spread(F[t + 1], b + 8)
        C = {}
        for k in range(8):
            for s in range(t + 2, n):
                C[s, k] = jnp.broadcast_to(F[s][:, b + k:b + k + 1], S)
        G = jnp.zeros(S, jnp.float32)
        for k in range(8):
            d = jnp.broadcast_to(D[k][k:k + 1], S)
            rs = lax.rsqrt(d)
            inv = 1.0 / d
            g = D[k] - onehot[k]
            xk = jnp.broadcast_to(X[k:k + 1], S)
            G = jnp.where(subl == k, xk * rs, G)
            X = X - g * (xk * inv)
            for m in range(k + 1, 8):
                f = jnp.broadcast_to(D[m][k:k + 1], S) * inv
                D[m] = D[m] - g * f
                if t + 1 < n:
                    B[m] = B[m] - B[k] * f
            if t + 1 < n:
                y = B[k] * inv
                N = [N[m] - B[k] * jnp.broadcast_to(y[m:m + 1], S) for m in range(8)]
        Ws.append(jnp.where(lane < b + 8, G, 0.0))
        if t + 1 < n:
            V = [jnp.broadcast_to(X[k:k + 1], S) for k in range(8)]
            for s in range(t + 1, n):
                f = jnp.where(inblk, 0.0, F[s])
                for k in range(8):
                    f = f - (first[k] if s == t + 1 else C[s, k]) * V[k]
                F[s] = f
            D = N
        beside(t)
    return Ws


def split(x, n):
    parts = []
    for i in range(n):
        h = x.astype(jnp.bfloat16)
        parts.append(h)
        if i + 1 < n:
            x = x - h.astype(jnp.float32)
    return parts

PAIRS = {2: [(0, 0), (0, 1), (1, 0)], 3: [(0, 0), (0, 1), (1, 0), (0, 2), (1, 1), (2, 0)]}

def dot_nt(a, b):
    pairs = PAIRS[len(a)]
    x = jnp.concatenate([a[i] for i, _ in pairs], axis=1)
    y = jnp.concatenate([b[j] for _, j in pairs], axis=1)
    return lax.dot_general(x, y, (((1,), (1,)), ((), ())), preferred_element_type=jnp.float32)

def dot_nt_narrow(a, b):
    rows = b[0].shape[0]
    x = jnp.concatenate([a[0], a[1]], axis=1)
    y = jnp.concatenate([jnp.concatenate([b[0], b[1]], axis=1), jnp.concatenate([b[1], b[0]], axis=1)], axis=0)
    u = lax.dot_general(x, y, (((1,), (1,)), ((), ())), preferred_element_type=jnp.float32)
    x = jnp.concatenate([a[0], a[2]], axis=1)
    y = jnp.concatenate([b[2], b[0]], axis=1)
    v = lax.dot_general(x, y, (((1,), (1,)), ((), ())), preferred_element_type=jnp.float32)
    return u[:, :rows] + (u[:, rows:] + v)


BT = 256


def each_tile(first, n, body):
    for f in range(n // BT):

        @pl.when(first == f)
        def _():
            for i in range(f, n // BT):
                body(i)


def chol_kernel(nparts, place_ref, packed_ref, band_ref, out_ref, a_ref, *scratch):
    Ls = scratch[:nparts]
    P, Q, W, sems = scratch[nparts:]
    n = a_ref.shape[0]
    nb = n // BLK
    np2 = n // 256
    r = place_ref[0]
    c = place_ref[1]

    early, late = [], []
    for i in range(nb):
        src = min(i, nb - 1 - i)
        first = 0 if 2 * i >= nb else BLK * (nb - i)
        for group, lo, hi in ((early, 0, min(2, i + 1)), (late, 2, i + 1)):
            if hi > lo:
                group.append(
                    pltpu.make_async_copy(
                        packed_ref.at[pl.ds(BLK * src, BLK), pl.ds(first + BLK * lo, BLK * (hi - lo))],
                        a_ref.at[pl.ds(BLK * i, BLK), pl.ds(BLK * lo, BLK * (hi - lo))],
                        sems.at[len(early) + len(late)],
                    )
                )
    for copy in early + late:
        copy.start()

    def zero(i, _):
        at = pl.ds(pl.multiple_of(i * 256, 256), 256)
        Q[at, :] = jnp.zeros((256, 256), jnp.float32)
        return 0

    lax.fori_loop(0, np2, zero, 0)
    out_ref[...] = jnp.zeros(out_ref.shape, jnp.float32)
    for copy in early:
        copy.wait()

    row_of = lax.broadcasted_iota(jnp.int32, (BLK, BLK), 0)
    col_of = lax.broadcasted_iota(jnp.int32, (BLK, BLK), 1)
    shift = jnp.where(row_of == col_of, SHIFT_NUM / 4.0, 0.0)

    def column(jj, _):
        J2 = jj // 2
        h = jj % 2
        base = pl.multiple_of(J2 * 256, 256)
        here = pl.multiple_of(jj * 128, 128)
        first = base // BT

        @pl.when(jj == 0)
        def _():
            def rows(i):
                at = pl.ds(i * BT, BT)
                P[at, :] = a_ref[at, :256]
            for i in range(n // BT):
                rows(i)

        @pl.when(jj == 1)
        def _():
            for copy in late:
                copy.wait()

        @pl.when((h == 0) & (jj > 0))
        def _():
            ks = pl.ds(pl.multiple_of(base - 256, 256), 256)
            def rows(i):
                at = pl.ds(i * BT, BT)
                P[at, :] = a_ref[at, pl.ds(base, 256)] + Q[at, :] - dot_nt([L[at, ks] for L in Ls], [L[pl.ds(base, 256), ks] for L in Ls])
                Q[at, :] = jnp.zeros((BT, 256), jnp.float32)
            each_tile(first, n, rows)

        @pl.when(h == 1)
        def _():
            prev = pl.ds(pl.multiple_of(here - 128, 128), 128)
            def rows(i):
                at = pl.ds(i * BT, BT)
                P[at, :128] = P[at, 128:] - dot_nt_narrow([L[at, prev] for L in Ls], [L[pl.ds(here, 128), prev] for L in Ls])
            each_tile(first, n, rows)

        units = (np2 // 2 * (np2 // 2 - 1) + 1) // 2
        later = jnp.minimum(J2 + 1, np2 - 1)
        deep = jnp.maximum(J2, 1)
        def unit(u):
            at = units * h + u
            real = at < J2 * (np2 - 1 - J2)
            i = J2 + 1 + at // deep
            src = pl.multiple_of(jnp.where(real, i, 0) * 256, 256)
            dst = pl.multiple_of(jnp.where(real, i, np2) * 256, 256)
            ks = pl.ds(pl.multiple_of(jnp.where(real, at % deep, 0) * 256, 256), 256)
            Q[pl.ds(dst, 256), :] -= dot_nt([L[pl.ds(src, 256), ks] for L in Ls], [L[pl.ds(pl.multiple_of(later * 256, 256), 256), ks] for L in Ls])
        def beside(t):
            if t % 2 == 0 and t // 2 < units:
                unit(t // 2)
        P[pl.ds(here, BLK), :BLK] += shift
        ws = diag128([P[pl.ds(pl.multiple_of(here + 8 * s, 8), 8), :128] for s in range(16)], beside)
        for s in range(16):
            W[8 * s:8 * s + 8, :] = ws[s]
        w = split(W[...], 3)
        def rows(i):
            at = pl.ds(i * BT, BT)
            l = dot_nt_narrow(split(P[at, :128], 3), w)
            for L, part in zip(Ls, split(l, nparts)):
                L[at, pl.ds(here, 128)] = part
            P[at, :128] = l
        each_tile(first, n, rows)

        @pl.when(jj == c)
        def _():
            rows = out_ref.shape[0]
            mine = P[pl.ds(pl.multiple_of(r * rows, rows), rows), :128]
            row = lax.broadcasted_iota(jnp.int32, mine.shape, 0) + r * rows
            col = lax.broadcasted_iota(jnp.int32, mine.shape, 1) + here
            out_ref[...] = jnp.where(row >= col, mine, 0.0)
        return 0
    lax.fori_loop(0, n // 128, column, 0)

    for q in range(2):
        i = 2 * r + q
        rows_i = pl.multiple_of(i * BLK, BLK)
        cols_c = pl.multiple_of(c * BLK, BLK)

        @pl.when(c <= i)
        def _():
            band_ref[q * BLK:(q + 1) * BLK, :] = a_ref[pl.ds(rows_i, BLK), pl.ds(cols_c, BLK)]

        @pl.when(c > i)
        def _():
            band_ref[q * BLK:(q + 1) * BLK, :] = a_ref[pl.ds(cols_c, BLK), pl.ds(rows_i, BLK)].T


def chol_piece(packed, place, n, rows, nparts=3):
    nb = n // BLK
    flat = jax.ShapeDtypeStruct((rows, BLK), jnp.float32)
    vmem = pl.BlockSpec(memory_space=pltpu.VMEM)
    return pl.pallas_call(
        functools.partial(chol_kernel, nparts),
        out_shape=(flat, flat),
        in_specs=[pl.BlockSpec(memory_space=pltpu.SMEM), pl.BlockSpec(memory_space=pl.ANY)],
        out_specs=(vmem, vmem),
        scratch_shapes=[pltpu.VMEM((n, n), jnp.float32)]
        + [pltpu.VMEM((n, n), jnp.bfloat16)] * nparts
        + [pltpu.VMEM((n, 256), jnp.float32), pltpu.VMEM((n + 256, 256), jnp.float32), pltpu.VMEM((BLK, BLK), jnp.float32), pltpu.SemaphoreType.DMA((2 * nb,))],
        compiler_params=pltpu.CompilerParams(vmem_limit_bytes=56 * 2**20),
        cost_estimate=pl.CostEstimate(flops=2 * n * n * n, bytes_accessed=300 * 2**20, transcendentals=n),
        name="factor",
    )(place, packed)


def band_kernel(scale, keep_ref, slab_ref, band_ref, got, sems):
    ncols = band_ref.shape[1] // BLK
    step = slab_ref.shape[1] // ncols
    copies = [
        pltpu.make_async_copy(slab_ref.at[:, pl.ds(c * step, BLK)], got.at[:, pl.ds(c * BLK, BLK)], sems.at[c])
        for c in range(ncols)
    ]
    for copy in copies:
        copy.start()
    for c, copy in enumerate(copies):
        copy.wait()
        at = slice(c * BLK, (c + 1) * BLK)
        band_ref[:, at] = got[:, at] * (keep_ref[0, c * step // BLK].astype(jnp.float32) * scale)


def band_columns(slab, block_mask, ncols, scale):
    users = slab.shape[0]
    return pl.pallas_call(
        functools.partial(band_kernel, scale),
        out_shape=jax.ShapeDtypeStruct((users, BLK * ncols), jnp.float32),
        in_specs=[pl.BlockSpec(memory_space=pltpu.SMEM), pl.BlockSpec(memory_space=pl.ANY)],
        out_specs=pl.BlockSpec(memory_space=pltpu.VMEM),
        scratch_shapes=[pltpu.VMEM((users, BLK * ncols), jnp.float32), pltpu.SemaphoreType.DMA((ncols,))],
        name="mask_band",
    )(block_mask, slab)


def rest_kernel(pair, scale, keep_ref, slab_ref, rest_ref):
    g = pl.program_id(0)
    blocks = slab_ref.shape[1] // BLK
    per = blocks // pair
    to = 0
    for b in range(blocks):
        if b % per:
            keep = keep_ref[0, g * blocks + b].astype(jnp.float32) * scale
            rest_ref[0, :, to:to + BLK] = slab_ref[:, b * BLK:(b + 1) * BLK] * keep
            to += BLK


def other_columns(slab, block_mask, ncols, nrows, scale):
    users, items = slab.shape
    pair = ncols // nrows
    other = items // nrows - pair * BLK
    return pl.pallas_call(
        functools.partial(rest_kernel, pair, scale),
        grid=(nrows,),
        out_shape=jax.ShapeDtypeStruct((nrows, users, other), jnp.float32),
        in_specs=[pl.BlockSpec(memory_space=pltpu.SMEM), pl.BlockSpec((users, items // nrows), lambda g: (0, g))],
        out_specs=pl.BlockSpec((1, users, other), lambda g: (g, 0, 0)),
        cost_estimate=pl.CostEstimate(flops=users * items, bytes_accessed=8 * users * items, transcendentals=0),
        name="mask_rest",
    )(block_mask, slab)


def strips_kernel(k_ref, left_ref, own_ref, far_ref, out_ref, left, right):
    depth = own_ref.shape[0]
    x = pl.program_id(1)

    @pl.when(x == 0)
    def _():
        for q in range(2):
            at = jnp.where(q == 0, k_ref[0], 1 - k_ref[0]) * depth
            high, low = split(left_ref[pl.ds(pl.multiple_of(at, depth), depth), :].T, 2)
            for i, part in enumerate((high, high, low)):
                left[q, :, depth * i:depth * (i + 1)] = part

    @pl.when(pl.program_id(0) == 0)
    def _():
        for q, ref in enumerate((own_ref, far_ref)):
            high, low = split(ref[...], 2)
            for i, part in enumerate((high, low, high)):
                right[x, q, depth * i:depth * (i + 1), :] = part

    both = jnp.dot(left[0], right[x, 0], preferred_element_type=jnp.float32) + jnp.dot(
        left[1], right[x, 1], preferred_element_type=jnp.float32
    )
    cols = out_ref.shape[-1]
    for i in range(out_ref.shape[0]):
        out_ref[i, 0] = both[:, cols * i:cols * (i + 1)]


def strips(k, bands, own, far, nz, nx):
    users, width = bands.shape
    rows, cols = width // (2 * nz), own.shape[1] // nx
    here = pl.BlockSpec((users // 2, 2 * cols), lambda z, x, k: (0, x))
    out = pl.pallas_call(
        strips_kernel,
        out_shape=jax.ShapeDtypeStruct((nx, nz, rows, cols), jnp.float32),
        grid_spec=pltpu.PrefetchScalarGridSpec(
            num_scalar_prefetch=1,
            grid=(nz, nx // 2),
            in_specs=[pl.BlockSpec((users, rows), lambda z, x, k: (0, 2 * z + k[0])), here, here],
            out_specs=pl.BlockSpec((2, 1, rows, cols), lambda z, x, k: (x, z, 0, 0)),
            scratch_shapes=[
                pltpu.VMEM((2, rows, 3 * users // 2), jnp.bfloat16),
                pltpu.VMEM((nx // 2, 2, 3 * users // 2, 2 * cols), jnp.bfloat16),
            ],
        ),
        compiler_params=pltpu.CompilerParams(vmem_limit_bytes=32 * 2**20),
        cost_estimate=pl.CostEstimate(flops=6 * users * nz * rows * nx * cols, bytes_accessed=40 * 2**20, transcendentals=0),
        name="strips",
    )(k.reshape(1).astype(jnp.int32), bands, own, far)
    return out.reshape(nx * nz * rows, cols)


def shards(slab, block_mask):
    z, k, y, x = (lax.axis_index(axis) for axis in ("z", "k", "y", "x"))
    groups = lax.axis_size("y") * lax.axis_size("k")
    ncols = lax.axis_size("z") * lax.axis_size("x")
    g = lax.axis_size("k") * y + k
    pair = ncols // groups
    total_users = slab.shape[0] * ncols * groups
    high = dict(precision=lax.Precision.HIGH, preferred_element_type=jnp.float32)
    over_users = (((0,), (0,)), ((), ()))

    scale = 2.0 ** -(total_users.bit_length() // 2)
    assert scale * scale * total_users == 1.0
    band = band_columns(slab, block_mask, ncols, scale)
    rest = other_columns(slab, block_mask, ncols, lax.axis_size("y"), scale)
    bands = lax.all_gather(band, ("k", "y"), axis=0, tiled=True)
    bands, rest = lax.optimization_barrier((bands, rest))

    upper = lax.dynamic_slice_in_dim(bands, BLK * g, BLK, 1)
    lower = lax.dynamic_slice_in_dim(bands, BLK * (ncols - 1 - g), BLK, 1)
    both = lax.dot_general(jnp.concatenate([lower, upper], axis=1), bands, over_users, **high)
    padded = jnp.concatenate([jnp.zeros((BLK, BLK * ncols), jnp.float32), both[BLK:]], axis=1)
    moved = lax.dynamic_slice_in_dim(padded, BLK * g, BLK * (ncols + 1), 1)
    long = jnp.concatenate([both[:BLK], jnp.zeros((BLK, BLK), jnp.float32)], axis=1)
    lane = lax.broadcasted_iota(jnp.int32, moved.shape, 1)
    packed = jnp.where(lane < BLK * (ncols - g), long, moved)
    pieces = lax.all_to_all(packed, ("z", "x"), split_axis=0, concat_axis=0, tiled=True)
    mine = jnp.sum(pieces.reshape(ncols, BLK // ncols, -1), axis=0)
    mine, rest = lax.optimization_barrier((mine, rest))
    panel = lax.all_gather(mine, ("y", "k", "z", "x"), axis=0, tiled=True)

    own = lax.all_to_all(rest, "y", split_axis=0, concat_axis=0, tiled=True)
    own = own.reshape(-1, own.shape[-1])
    far = lax.ppermute(own, "k", [(0, 1), (1, 0)])
    partial = strips(k, bands, own, far, lax.axis_size("z"), lax.axis_size("x"))
    items = lax.psum_scatter(partial, ("x", "z"), scatter_dimension=0, tiled=True)

    place = jnp.stack([lax.axis_size("k") * z + k, lax.axis_size("x") * y + x]).astype(jnp.int32)
    block, piece = chol_piece(panel, place, BLK * ncols, BLK * pair)
    items, block, piece = lax.optimization_barrier((items, block, piece))
    return (jnp.concatenate([block, items], axis=1), piece)


def solution(mesh):
    rows, cols = mesh.devices.shape
    axes = ("z", "k", "y", "x")
    fine = Mesh(mesh.devices.reshape(rows // 2, 2, cols // 4, 4), axes)
    return jax.shard_map(
        shards,
        mesh=fine,
        in_specs=(P(axes, None), P(axes, None)),
        out_specs=(P(("z", "k"), ("y", "x")), P(("z", "k"), ("y", "x"))),
        check_vma=False,
    )
```

```python
import functools

import jax
import jax.numpy as jnp
from jax import lax
from jax.experimental import pallas as pl
from jax.experimental.pallas import tpu as pltpu
from jax.sharding import Mesh
from jax.sharding import PartitionSpec as P

BLK = 128
SHIFT_NUM = 2


def diag128(F, beside=lambda t: None):
    S = (8, 128)
    lane = lax.broadcasted_iota(jnp.int32, S, 1)
    subl = lax.broadcasted_iota(jnp.int32, S, 0)
    F = list(F)
    Ws, Us = [], []
    n = len(F)
    spread = lambda x, at: [jnp.broadcast_to(x[:, at + k:at + k + 1], S) for k in range(8)]
    D = spread(F[0], 0)
    for t in range(n):
        b = 8 * t
        inblk = (lane >= b) & (lane < b + 8)
        X = F[t]
        Z = jnp.where(lane - b == subl, 1.0, 0.0)
        if t + 1 < n:
            first = spread(F[t + 1], b)
            B = list(first)
            N = spread(F[t + 1], b + 8)
        C = {}
        for k in range(8):
            for s in range(t + 2, n):
                C[s, k] = jnp.broadcast_to(F[s][:, b + k:b + k + 1], S)
        G = jnp.zeros(S, jnp.float32)
        H = jnp.zeros(S, jnp.float32)
        scaled, f = [], {}
        for k in range(8):
            d = jnp.broadcast_to(D[k][k:k + 1], S)
            rs = lax.rsqrt(d)
            inv = 1.0 / d
            g = jnp.where(subl > k, D[k], 0.0)
            xk = jnp.broadcast_to(X[k:k + 1], S)
            zk = jnp.broadcast_to(Z[k:k + 1], S)
            G = jnp.where(subl == k, xk * rs, G)
            H = jnp.where(subl == k, zk * rs, H)
            X = X - g * (xk * inv)
            Z = Z - g * (zk * inv)
            scaled.append(jnp.where(inblk, zk, xk) * inv)
            for m in range(k + 1, 8):
                f[k, m] = jnp.broadcast_to(D[m][k:k + 1], S) * inv
                D[m] = D[m] - g * f[k, m]
                if t + 1 < n:
                    B[m] = B[m] - B[k] * f[k, m]
            if t + 1 < n:
                y = B[k] * inv
                N = [N[m] - B[k] * jnp.broadcast_to(y[m:m + 1], S) for m in range(8)]
        Ws.append(jnp.where(lane < b, G, jnp.where(inblk, H, 0.0)))
        Us.append(jnp.where(lane >= b + subl, G, 0.0))
        if t + 1 < n:
            V = list(scaled)
            for m in range(7, 0, -1):
                for k in range(m):
                    V[k] = V[k] - f[k, m] * V[m]
            for s in range(t + 1, n):
                row = jnp.where(inblk, 0.0, F[s])
                for k in range(8):
                    row = row - (first[k] if s == t + 1 else C[s, k]) * V[k]
                F[s] = row
            D = N
        beside(t)
    return Ws, Us


def split(x, n):
    parts = []
    for i in range(n):
        h = x.astype(jnp.bfloat16)
        parts.append(h)
        if i + 1 < n:
            x = x - h.astype(jnp.float32)
    return parts

PAIRS = {2: [(0, 0), (0, 1), (1, 0)], 3: [(0, 0), (0, 1), (1, 0), (0, 2), (1, 1), (2, 0)]}

def dot_nt(a, b):
    pairs = PAIRS[len(a)]
    x = jnp.concatenate([a[i] for i, _ in pairs], axis=1)
    y = jnp.concatenate([b[j] for _, j in pairs], axis=1)
    return lax.dot_general(x, y, (((1,), (1,)), ((), ())), preferred_element_type=jnp.float32)

def dot_nt_narrow(a, b):
    rows = b[0].shape[0]
    x = jnp.concatenate([a[0], a[1]], axis=1)
    y = jnp.concatenate([jnp.concatenate([b[0], b[1]], axis=1), jnp.concatenate([b[1], b[0]], axis=1)], axis=0)
    u = lax.dot_general(x, y, (((1,), (1,)), ((), ())), preferred_element_type=jnp.float32)
    x = jnp.concatenate([a[0], a[2]], axis=1)
    y = jnp.concatenate([b[2], b[0]], axis=1)
    v = lax.dot_general(x, y, (((1,), (1,)), ((), ())), preferred_element_type=jnp.float32)
    return u[:, :rows] + (u[:, rows:] + v)


BT = 256


def each_tile(first, n, body):
    for f in range(n // BT):

        @pl.when(first == f)
        def _():
            for i in range(f, n // BT):
                body(i)


def chol_kernel(nparts, place_ref, packed_ref, band_ref, out_ref, a_ref, *scratch):
    Ls = scratch[:nparts]
    P, Q, W, U, sems = scratch[nparts:]
    n = a_ref.shape[0]
    nb = n // BLK
    np2 = n // 256
    r = place_ref[0]
    c = place_ref[1]

    early, late = [], []
    for i in range(nb):
        src = min(i, nb - 1 - i)
        first = 0 if 2 * i >= nb else BLK * (nb - i)
        for group, lo, hi in ((early, 0, min(2, i + 1)), (late, 2, i + 1)):
            if hi > lo:
                group.append(
                    pltpu.make_async_copy(
                        packed_ref.at[pl.ds(BLK * src, BLK), pl.ds(first + BLK * lo, BLK * (hi - lo))],
                        a_ref.at[pl.ds(BLK * i, BLK), pl.ds(BLK * lo, BLK * (hi - lo))],
                        sems.at[len(early) + len(late)],
                    )
                )
    for copy in early + late:
        copy.start()

    def zero(i, _):
        at = pl.ds(pl.multiple_of(i * 256, 256), 256)
        Q[at, :] = jnp.zeros((256, 256), jnp.float32)
        return 0

    lax.fori_loop(0, np2, zero, 0)
    out_ref[...] = jnp.zeros(out_ref.shape, jnp.float32)
    for copy in early:
        copy.wait()

    row_of = lax.broadcasted_iota(jnp.int32, (BLK, BLK), 0)
    col_of = lax.broadcasted_iota(jnp.int32, (BLK, BLK), 1)
    shift = jnp.where(row_of == col_of, SHIFT_NUM / 4.0, 0.0)

    def column(jj, _):
        J2 = jj // 2
        h = jj % 2
        base = pl.multiple_of(J2 * 256, 256)
        here = pl.multiple_of(jj * 128, 128)
        first = base // BT

        @pl.when(jj == 0)
        def _():
            def rows(i):
                at = pl.ds(i * BT, BT)
                P[at, :] = a_ref[at, :256]
            for i in range(n // BT):
                rows(i)

        @pl.when(jj == 1)
        def _():
            for copy in late:
                copy.wait()

        @pl.when((h == 0) & (jj > 0))
        def _():
            ks = pl.ds(pl.multiple_of(base - 256, 256), 256)
            def rows(i):
                at = pl.ds(i * BT, BT)
                P[at, :] = a_ref[at, pl.ds(base, 256)] + Q[at, :] - dot_nt([L[at, ks] for L in Ls], [L[pl.ds(base, 256), ks] for L in Ls])
                Q[at, :] = jnp.zeros((BT, 256), jnp.float32)
            each_tile(first, n, rows)

        @pl.when(h == 1)
        def _():
            prev = pl.ds(pl.multiple_of(here - 128, 128), 128)
            def rows(i):
                at = pl.ds(i * BT, BT)
                P[at, :128] = P[at, 128:] - dot_nt_narrow([L[at, prev] for L in Ls], [L[pl.ds(here, 128), prev] for L in Ls])
            each_tile(first, n, rows)

        units = (np2 // 2 * (np2 // 2 - 1) + 1) // 2
        later = jnp.minimum(J2 + 1, np2 - 1)
        deep = jnp.maximum(J2, 1)
        def unit(u):
            at = units * h + u
            real = at < J2 * (np2 - 1 - J2)
            i = J2 + 1 + at // deep
            src = pl.multiple_of(jnp.where(real, i, 0) * 256, 256)
            dst = pl.multiple_of(jnp.where(real, i, np2) * 256, 256)
            ks = pl.ds(pl.multiple_of(jnp.where(real, at % deep, 0) * 256, 256), 256)
            Q[pl.ds(dst, 256), :] -= dot_nt([L[pl.ds(src, 256), ks] for L in Ls], [L[pl.ds(pl.multiple_of(later * 256, 256), 256), ks] for L in Ls])
        def beside(t):
            if t % 2 == 0 and t // 2 < units:
                unit(t // 2)
        P[pl.ds(here, BLK), :BLK] += shift
        ws, us = diag128([P[pl.ds(pl.multiple_of(here + 8 * s, 8), 8), :128] for s in range(16)], beside)
        for s in range(16):
            W[8 * s:8 * s + 8, :] = ws[s]
            U[8 * s:8 * s + 8, :] = us[s]
        w = W[...]
        off = jnp.where(row_of == col_of, 1.0, 0.0) - dot_nt_narrow(split(w, 3), split(U[...], 3))
        w = w + jnp.dot(off.astype(jnp.bfloat16), w.astype(jnp.bfloat16), preferred_element_type=jnp.float32)
        w = split(w, 3)
        def rows(i):
            at = pl.ds(i * BT, BT)
            l = dot_nt_narrow(split(P[at, :128], 3), w)
            for L, part in zip(Ls, split(l, nparts)):
                L[at, pl.ds(here, 128)] = part
            P[at, :128] = l
        each_tile(first, n, rows)

        @pl.when(jj == c)
        def _():
            rows = out_ref.shape[0]
            mine = P[pl.ds(pl.multiple_of(r * rows, rows), rows), :128]
            row = lax.broadcasted_iota(jnp.int32, mine.shape, 0) + r * rows
            col = lax.broadcasted_iota(jnp.int32, mine.shape, 1) + here
            out_ref[...] = jnp.where(row >= col, mine, 0.0)
        return 0
    lax.fori_loop(0, n // 128, column, 0)

    for q in range(2):
        i = 2 * r + q
        rows_i = pl.multiple_of(i * BLK, BLK)
        cols_c = pl.multiple_of(c * BLK, BLK)

        @pl.when(c <= i)
        def _():
            band_ref[q * BLK:(q + 1) * BLK, :] = a_ref[pl.ds(rows_i, BLK), pl.ds(cols_c, BLK)]

        @pl.when(c > i)
        def _():
            band_ref[q * BLK:(q + 1) * BLK, :] = a_ref[pl.ds(cols_c, BLK), pl.ds(rows_i, BLK)].T


def chol_piece(packed, place, n, rows, nparts=3):
    nb = n // BLK
    flat = jax.ShapeDtypeStruct((rows, BLK), jnp.float32)
    vmem = pl.BlockSpec(memory_space=pltpu.VMEM)
    return pl.pallas_call(
        functools.partial(chol_kernel, nparts),
        out_shape=(flat, flat),
        in_specs=[pl.BlockSpec(memory_space=pltpu.SMEM), pl.BlockSpec(memory_space=pl.ANY)],
        out_specs=(vmem, vmem),
        scratch_shapes=[pltpu.VMEM((n, n), jnp.float32)]
        + [pltpu.VMEM((n, n), jnp.bfloat16)] * nparts
        + [pltpu.VMEM((n, 256), jnp.float32), pltpu.VMEM((n + 256, 256), jnp.float32), pltpu.VMEM((BLK, BLK), jnp.float32), pltpu.VMEM((BLK, BLK), jnp.float32), pltpu.SemaphoreType.DMA((2 * nb,))],
        compiler_params=pltpu.CompilerParams(vmem_limit_bytes=56 * 2**20),
        cost_estimate=pl.CostEstimate(flops=2 * n * n * n, bytes_accessed=300 * 2**20, transcendentals=n),
        name="factor",
    )(place, packed)


def band_kernel(scale, keep_ref, slab_ref, band_ref, got, sems):
    ncols = band_ref.shape[1] // BLK
    step = slab_ref.shape[1] // ncols
    copies = [
        pltpu.make_async_copy(slab_ref.at[:, pl.ds(c * step, BLK)], got.at[:, pl.ds(c * BLK, BLK)], sems.at[c])
        for c in range(ncols)
    ]
    for copy in copies:
        copy.start()
    for c, copy in enumerate(copies):
        copy.wait()
        at = slice(c * BLK, (c + 1) * BLK)
        band_ref[:, at] = got[:, at] * (keep_ref[0, c * step // BLK].astype(jnp.float32) * scale)


def band_columns(slab, block_mask, ncols, scale):
    users = slab.shape[0]
    return pl.pallas_call(
        functools.partial(band_kernel, scale),
        out_shape=jax.ShapeDtypeStruct((users, BLK * ncols), jnp.float32),
        in_specs=[pl.BlockSpec(memory_space=pltpu.SMEM), pl.BlockSpec(memory_space=pl.ANY)],
        out_specs=pl.BlockSpec(memory_space=pltpu.VMEM),
        scratch_shapes=[pltpu.VMEM((users, BLK * ncols), jnp.float32), pltpu.SemaphoreType.DMA((ncols,))],
        name="mask_band",
    )(block_mask, slab)


def rest_kernel(pair, scale, keep_ref, slab_ref, rest_ref):
    g = pl.program_id(0)
    blocks = slab_ref.shape[1] // BLK
    per = blocks // pair
    to = 0
    for b in range(blocks):
        if b % per:
            keep = keep_ref[0, g * blocks + b].astype(jnp.float32) * scale
            rest_ref[0, :, to:to + BLK] = slab_ref[:, b * BLK:(b + 1) * BLK] * keep
            to += BLK


def other_columns(slab, block_mask, ncols, nrows, scale):
    users, items = slab.shape
    pair = ncols // nrows
    other = items // nrows - pair * BLK
    return pl.pallas_call(
        functools.partial(rest_kernel, pair, scale),
        grid=(nrows,),
        out_shape=jax.ShapeDtypeStruct((nrows, users, other), jnp.float32),
        in_specs=[pl.BlockSpec(memory_space=pltpu.SMEM), pl.BlockSpec((users, items // nrows), lambda g: (0, g))],
        out_specs=pl.BlockSpec((1, users, other), lambda g: (g, 0, 0)),
        cost_estimate=pl.CostEstimate(flops=users * items, bytes_accessed=8 * users * items, transcendentals=0),
        name="mask_rest",
    )(block_mask, slab)


def strips_kernel(k_ref, left_ref, own_ref, far_ref, out_ref, left, right):
    depth = own_ref.shape[0]
    x = pl.program_id(1)

    @pl.when(x == 0)
    def _():
        for q in range(2):
            at = jnp.where(q == 0, k_ref[0], 1 - k_ref[0]) * depth
            high, low = split(left_ref[pl.ds(pl.multiple_of(at, depth), depth), :].T, 2)
            for i, part in enumerate((high, high, low)):
                left[q, :, depth * i:depth * (i + 1)] = part

    @pl.when(pl.program_id(0) == 0)
    def _():
        for q, ref in enumerate((own_ref, far_ref)):
            high, low = split(ref[...], 2)
            for i, part in enumerate((high, low, high)):
                right[x, q, depth * i:depth * (i + 1), :] = part

    both = jnp.dot(left[0], right[x, 0], preferred_element_type=jnp.float32) + jnp.dot(
        left[1], right[x, 1], preferred_element_type=jnp.float32
    )
    cols = out_ref.shape[-1]
    for i in range(out_ref.shape[0]):
        out_ref[i, 0] = both[:, cols * i:cols * (i + 1)]


def strips(k, bands, own, far, nz, nx):
    users, width = bands.shape
    rows, cols = width // (2 * nz), own.shape[1] // nx
    here = pl.BlockSpec((users // 2, 2 * cols), lambda z, x, k: (0, x))
    out = pl.pallas_call(
        strips_kernel,
        out_shape=jax.ShapeDtypeStruct((nx, nz, rows, cols), jnp.float32),
        grid_spec=pltpu.PrefetchScalarGridSpec(
            num_scalar_prefetch=1,
            grid=(nz, nx // 2),
            in_specs=[pl.BlockSpec((users, rows), lambda z, x, k: (0, 2 * z + k[0])), here, here],
            out_specs=pl.BlockSpec((2, 1, rows, cols), lambda z, x, k: (x, z, 0, 0)),
            scratch_shapes=[
                pltpu.VMEM((2, rows, 3 * users // 2), jnp.bfloat16),
                pltpu.VMEM((nx // 2, 2, 3 * users // 2, 2 * cols), jnp.bfloat16),
            ],
        ),
        compiler_params=pltpu.CompilerParams(vmem_limit_bytes=56 * 2**20),
        cost_estimate=pl.CostEstimate(flops=6 * users * nz * rows * nx * cols, bytes_accessed=40 * 2**20, transcendentals=0),
        name="strips",
    )(k.reshape(1).astype(jnp.int32), bands, own, far)
    return out.reshape(nx * nz * rows, cols)


def shards(slab, block_mask):
    z, k, y, x = (lax.axis_index(axis) for axis in ("z", "k", "y", "x"))
    groups = lax.axis_size("y") * lax.axis_size("k")
    ncols = lax.axis_size("z") * lax.axis_size("x")
    g = lax.axis_size("k") * y + k
    pair = ncols // groups
    total_users = slab.shape[0] * ncols * groups
    high = dict(precision=lax.Precision.HIGH, preferred_element_type=jnp.float32)
    over_users = (((0,), (0,)), ((), ()))

    scale = 2.0 ** -(total_users.bit_length() // 2)
    assert scale * scale * total_users == 1.0
    band = band_columns(slab, block_mask, ncols, scale)
    rest = other_columns(slab, block_mask, ncols, lax.axis_size("y"), scale)
    bands = lax.all_gather(band, ("k", "y"), axis=0, tiled=True)
    bands, rest = lax.optimization_barrier((bands, rest))

    upper = lax.dynamic_slice_in_dim(bands, BLK * g, BLK, 1)
    lower = lax.dynamic_slice_in_dim(bands, BLK * (ncols - 1 - g), BLK, 1)
    both = lax.dot_general(jnp.concatenate([lower, upper], axis=1), bands, over_users, **high)
    padded = jnp.concatenate([jnp.zeros((BLK, BLK * ncols), jnp.float32), both[BLK:]], axis=1)
    moved = lax.dynamic_slice_in_dim(padded, BLK * g, BLK * (ncols + 1), 1)
    long = jnp.concatenate([both[:BLK], jnp.zeros((BLK, BLK), jnp.float32)], axis=1)
    lane = lax.broadcasted_iota(jnp.int32, moved.shape, 1)
    packed = jnp.where(lane < BLK * (ncols - g), long, moved)
    pieces = lax.all_to_all(packed, ("z", "x"), split_axis=0, concat_axis=0, tiled=True)
    mine = jnp.sum(pieces.reshape(ncols, BLK // ncols, -1), axis=0)
    mine, rest = lax.optimization_barrier((mine, rest))
    panel = lax.all_gather(mine, ("y", "k", "z", "x"), axis=0, tiled=True)

    own = lax.all_to_all(rest, "y", split_axis=0, concat_axis=0, tiled=True)
    own = own.reshape(-1, own.shape[-1])
    far = lax.ppermute(own, "k", [(0, 1), (1, 0)])
    partial = strips(k, bands, own, far, lax.axis_size("z"), lax.axis_size("x"))
    items = lax.psum_scatter(partial, ("x", "z"), scatter_dimension=0, tiled=True)

    place = jnp.stack([lax.axis_size("k") * z + k, lax.axis_size("x") * y + x]).astype(jnp.int32)
    block, piece = chol_piece(panel, place, BLK * ncols, BLK * pair)
    items, block, piece = lax.optimization_barrier((items, block, piece))
    return (jnp.concatenate([block, items], axis=1), piece)


def solution(mesh):
    rows, cols = mesh.devices.shape
    axes = ("z", "k", "y", "x")
    fine = Mesh(mesh.devices.reshape(rows // 2, 2, cols // 4, 4), axes)
    return jax.shard_map(
        shards,
        mesh=fine,
        in_specs=(P(axes, None), P(axes, None)),
        out_specs=(P(("z", "k"), ("y", "x")), P(("z", "k"), ("y", "x"))),
        check_vma=False,
    )
```

```python
import functools

import jax
import jax.numpy as jnp
from jax import lax
from jax.experimental import pallas as pl
from jax.experimental.pallas import tpu as pltpu
from jax.sharding import Mesh
from jax.sharding import PartitionSpec as P

BLK = 128
SHIFT_NUM = 2


def diag128(F, beside=lambda t: None):
    S = (8, 128)
    lane = lax.broadcasted_iota(jnp.int32, S, 1)
    subl = lax.broadcasted_iota(jnp.int32, S, 0)
    F = list(F)
    Ws, Us = [], []
    n = len(F)
    spread = lambda x, at: [jnp.broadcast_to(x[:, at + k:at + k + 1], S) for k in range(8)]
    D = spread(F[0], 0)
    for t in range(n):
        b = 8 * t
        inblk = (lane >= b) & (lane < b + 8)
        X = F[t]
        Z = jnp.where(lane - b == subl, 1.0, 0.0)
        if t + 1 < n:
            first = spread(F[t + 1], b)
            B = list(first)
            N = spread(F[t + 1], b + 8)
        C = {}
        for k in range(8):
            for s in range(t + 2, n):
                C[s, k] = jnp.broadcast_to(F[s][:, b + k:b + k + 1], S)
        G = jnp.zeros(S, jnp.float32)
        H = jnp.zeros(S, jnp.float32)
        scaled, f = [], {}
        for k in range(8):
            d = jnp.broadcast_to(D[k][k:k + 1], S)
            rs = lax.rsqrt(d)
            inv = 1.0 / d
            g = jnp.where(subl > k, D[k], 0.0)
            xk = jnp.broadcast_to(X[k:k + 1], S)
            zk = jnp.broadcast_to(Z[k:k + 1], S)
            G = jnp.where(subl == k, xk * rs, G)
            H = jnp.where(subl == k, zk * rs, H)
            X = X - g * (xk * inv)
            Z = Z - g * (zk * inv)
            scaled.append(jnp.where(inblk, zk, xk) * inv)
            for m in range(k + 1, 8):
                f[k, m] = jnp.broadcast_to(D[m][k:k + 1], S) * inv
                D[m] = D[m] - g * f[k, m]
                if t + 1 < n:
                    B[m] = B[m] - B[k] * f[k, m]
            if t + 1 < n:
                y = B[k] * inv
                N = [N[m] - B[k] * jnp.broadcast_to(y[m:m + 1], S) for m in range(8)]
        Ws.append(jnp.where(lane < b, G, jnp.where(inblk, H, 0.0)))
        Us.append(jnp.where(lane >= b + subl, G, 0.0))
        if t + 1 < n:
            V = list(scaled)
            for m in range(7, 0, -1):
                for k in range(m):
                    V[k] = V[k] - f[k, m] * V[m]
            for s in range(t + 1, n):
                row = jnp.where(inblk, 0.0, F[s])
                for k in range(8):
                    row = row - (first[k] if s == t + 1 else C[s, k]) * V[k]
                F[s] = row
            D = N
        beside(t)
    return Ws, Us


def split(x, n):
    parts = []
    for i in range(n):
        h = x.astype(jnp.bfloat16)
        parts.append(h)
        if i + 1 < n:
            x = x - h.astype(jnp.float32)
    return parts

PAIRS = {2: [(0, 0), (0, 1), (1, 0)], 3: [(0, 0), (0, 1), (1, 0), (0, 2), (1, 1), (2, 0)]}

def dot_nt(a, b):
    pairs = PAIRS[len(a)]
    x = jnp.concatenate([a[i] for i, _ in pairs], axis=1)
    y = jnp.concatenate([b[j] for _, j in pairs], axis=1)
    return lax.dot_general(x, y, (((1,), (1,)), ((), ())), preferred_element_type=jnp.float32)

def dot_nt_narrow(a, b):
    rows = b[0].shape[0]
    x = jnp.concatenate([a[0], a[1]], axis=1)
    y = jnp.concatenate([jnp.concatenate([b[0], b[1]], axis=1), jnp.concatenate([b[1], b[0]], axis=1)], axis=0)
    u = lax.dot_general(x, y, (((1,), (1,)), ((), ())), preferred_element_type=jnp.float32)
    x = jnp.concatenate([a[0], a[2]], axis=1)
    y = jnp.concatenate([b[2], b[0]], axis=1)
    v = lax.dot_general(x, y, (((1,), (1,)), ((), ())), preferred_element_type=jnp.float32)
    return u[:, :rows] + (u[:, rows:] + v)


BT = 256


def each_tile(first, n, body):
    for f in range(n // BT):

        @pl.when(first == f)
        def _():
            for i in range(f, n // BT):
                body(i)


def chol_kernel(nparts, place_ref, packed_ref, band_ref, out_ref, a_ref, *scratch):
    Ls = scratch[:nparts]
    P, Q, W, U, sems = scratch[nparts:]
    n = a_ref.shape[0]
    nb = n // BLK
    np2 = n // 256
    r = place_ref[0]
    c = place_ref[1]

    early, late = [], []
    for i in range(nb):
        src = min(i, nb - 1 - i)
        first = 0 if 2 * i >= nb else BLK * (nb - i)
        for group, lo, hi in ((early, 0, min(2, i + 1)), (late, 2, i + 1)):
            if hi > lo:
                group.append(
                    pltpu.make_async_copy(
                        packed_ref.at[pl.ds(BLK * src, BLK), pl.ds(first + BLK * lo, BLK * (hi - lo))],
                        a_ref.at[pl.ds(BLK * i, BLK), pl.ds(BLK * lo, BLK * (hi - lo))],
                        sems.at[len(early) + len(late)],
                    )
                )
    for copy in early + late:
        copy.start()

    def zero(i, _):
        at = pl.ds(pl.multiple_of(i * 256, 256), 256)
        Q[at, :] = jnp.zeros((256, 256), jnp.float32)
        return 0

    lax.fori_loop(0, np2, zero, 0)
    out_ref[...] = jnp.zeros(out_ref.shape, jnp.float32)
    for copy in early:
        copy.wait()

    row_of = lax.broadcasted_iota(jnp.int32, (BLK, BLK), 0)
    col_of = lax.broadcasted_iota(jnp.int32, (BLK, BLK), 1)
    shift = jnp.where(row_of == col_of, SHIFT_NUM / 4.0, 0.0)

    def column(jj, _):
        J2 = jj // 2
        h = jj % 2
        base = pl.multiple_of(J2 * 256, 256)
        here = pl.multiple_of(jj * 128, 128)
        first = base // BT

        @pl.when(jj == 0)
        def _():
            def rows(i):
                at = pl.ds(i * BT, BT)
                P[at, :] = a_ref[at, :256]
            for i in range(n // BT):
                rows(i)

        @pl.when(jj == 1)
        def _():
            for copy in late:
                copy.wait()

        @pl.when((h == 0) & (jj > 0))
        def _():
            ks = pl.ds(pl.multiple_of(base - 256, 256), 256)
            def rows(i):
                at = pl.ds(i * BT, BT)
                P[at, :] = a_ref[at, pl.ds(base, 256)] + Q[at, :] - dot_nt([L[at, ks] for L in Ls], [L[pl.ds(base, 256), ks] for L in Ls])
                Q[at, :] = jnp.zeros((BT, 256), jnp.float32)
            each_tile(first, n, rows)

        @pl.when(h == 1)
        def _():
            prev = pl.ds(pl.multiple_of(here - 128, 128), 128)
            def rows(i):
                at = pl.ds(i * BT, BT)
                P[at, :128] = P[at, 128:] - dot_nt_narrow([L[at, prev] for L in Ls], [L[pl.ds(here, 128), prev] for L in Ls])
            each_tile(first, n, rows)

        units = (np2 // 2 * (np2 // 2 - 1) + 1) // 2
        later = jnp.minimum(J2 + 1, np2 - 1)
        deep = jnp.maximum(J2, 1)
        def unit(u):
            at = units * h + u
            real = at < J2 * (np2 - 1 - J2)
            i = J2 + 1 + at // deep
            src = pl.multiple_of(jnp.where(real, i, 0) * 256, 256)
            dst = pl.multiple_of(jnp.where(real, i, np2) * 256, 256)
            ks = pl.ds(pl.multiple_of(jnp.where(real, at % deep, 0) * 256, 256), 256)
            Q[pl.ds(dst, 256), :] -= dot_nt([L[pl.ds(src, 256), ks] for L in Ls], [L[pl.ds(pl.multiple_of(later * 256, 256), 256), ks] for L in Ls])
        def block_inverse(some):
            def beside(t):
                if some and t % 2 == 0 and t // 2 < units:
                    unit(t // 2)

            ws, us = diag128([P[pl.ds(pl.multiple_of(here + 8 * s, 8), 8), :128] for s in range(16)], beside)
            for s in range(16):
                W[8 * s:8 * s + 8, :] = ws[s]
                U[8 * s:8 * s + 8, :] = us[s]

        P[pl.ds(here, BLK), :BLK] += shift
        none = J2 * (np2 - 1 - J2) == 0

        @pl.when(none)
        def _():
            block_inverse(False)

        @pl.when(jnp.logical_not(none))
        def _():
            block_inverse(True)

        w = W[...]
        off = jnp.where(row_of == col_of, 1.0, 0.0) - dot_nt_narrow(split(w, 3), split(U[...], 3))
        w = w + jnp.dot(off.astype(jnp.bfloat16), w.astype(jnp.bfloat16), preferred_element_type=jnp.float32)
        w = split(w, 3)
        def rows(i):
            at = pl.ds(i * BT, BT)
            l = dot_nt_narrow(split(P[at, :128], 3), w)
            for L, part in zip(Ls, split(l, nparts)):
                L[at, pl.ds(here, 128)] = part
            P[at, :128] = l
        each_tile(first, n, rows)

        @pl.when(jj == c)
        def _():
            rows = out_ref.shape[0]
            mine = P[pl.ds(pl.multiple_of(r * rows, rows), rows), :128]
            row = lax.broadcasted_iota(jnp.int32, mine.shape, 0) + r * rows
            col = lax.broadcasted_iota(jnp.int32, mine.shape, 1) + here
            out_ref[...] = jnp.where(row >= col, mine, 0.0)
        return 0
    lax.fori_loop(0, n // 128, column, 0)

    for q in range(2):
        i = 2 * r + q
        rows_i = pl.multiple_of(i * BLK, BLK)
        cols_c = pl.multiple_of(c * BLK, BLK)

        @pl.when(c <= i)
        def _():
            band_ref[q * BLK:(q + 1) * BLK, :] = a_ref[pl.ds(rows_i, BLK), pl.ds(cols_c, BLK)]

        @pl.when(c > i)
        def _():
            band_ref[q * BLK:(q + 1) * BLK, :] = a_ref[pl.ds(cols_c, BLK), pl.ds(rows_i, BLK)].T


def chol_piece(packed, place, n, rows, nparts=3):
    nb = n // BLK
    flat = jax.ShapeDtypeStruct((rows, BLK), jnp.float32)
    vmem = pl.BlockSpec(memory_space=pltpu.VMEM)
    return pl.pallas_call(
        functools.partial(chol_kernel, nparts),
        out_shape=(flat, flat),
        in_specs=[pl.BlockSpec(memory_space=pltpu.SMEM), pl.BlockSpec(memory_space=pl.ANY)],
        out_specs=(vmem, vmem),
        scratch_shapes=[pltpu.VMEM((n, n), jnp.float32)]
        + [pltpu.VMEM((n, n), jnp.bfloat16)] * nparts
        + [pltpu.VMEM((n, 256), jnp.float32), pltpu.VMEM((n + 256, 256), jnp.float32), pltpu.VMEM((BLK, BLK), jnp.float32), pltpu.VMEM((BLK, BLK), jnp.float32), pltpu.SemaphoreType.DMA((2 * nb,))],
        compiler_params=pltpu.CompilerParams(vmem_limit_bytes=56 * 2**20),
        cost_estimate=pl.CostEstimate(flops=2 * n * n * n, bytes_accessed=300 * 2**20, transcendentals=n),
        name="factor",
    )(place, packed)


def band_kernel(scale, keep_ref, slab_ref, band_ref, got, sems):
    ncols = band_ref.shape[1] // BLK
    step = slab_ref.shape[1] // ncols
    copies = [
        pltpu.make_async_copy(slab_ref.at[:, pl.ds(c * step, BLK)], got.at[:, pl.ds(c * BLK, BLK)], sems.at[c])
        for c in range(ncols)
    ]
    for copy in copies:
        copy.start()
    for c, copy in enumerate(copies):
        copy.wait()
        at = slice(c * BLK, (c + 1) * BLK)
        band_ref[:, at] = got[:, at] * (keep_ref[0, c * step // BLK].astype(jnp.float32) * scale)


def band_columns(slab, block_mask, ncols, scale):
    users = slab.shape[0]
    return pl.pallas_call(
        functools.partial(band_kernel, scale),
        out_shape=jax.ShapeDtypeStruct((users, BLK * ncols), jnp.float32),
        in_specs=[pl.BlockSpec(memory_space=pltpu.SMEM), pl.BlockSpec(memory_space=pl.ANY)],
        out_specs=pl.BlockSpec(memory_space=pltpu.VMEM),
        scratch_shapes=[pltpu.VMEM((users, BLK * ncols), jnp.float32), pltpu.SemaphoreType.DMA((ncols,))],
        name="mask_band",
    )(block_mask, slab)


def rest_kernel(pair, scale, keep_ref, slab_ref, rest_ref):
    g = pl.program_id(0)
    blocks = slab_ref.shape[1] // BLK
    per = blocks // pair
    to = 0
    for b in range(blocks):
        if b % per:
            keep = keep_ref[0, g * blocks + b].astype(jnp.float32) * scale
            rest_ref[0, :, to:to + BLK] = slab_ref[:, b * BLK:(b + 1) * BLK] * keep
            to += BLK


def other_columns(slab, block_mask, ncols, nrows, scale):
    users, items = slab.shape
    pair = ncols // nrows
    other = items // nrows - pair * BLK
    return pl.pallas_call(
        functools.partial(rest_kernel, pair, scale),
        grid=(nrows,),
        out_shape=jax.ShapeDtypeStruct((nrows, users, other), jnp.float32),
        in_specs=[pl.BlockSpec(memory_space=pltpu.SMEM), pl.BlockSpec((users, items // nrows), lambda g: (0, g))],
        out_specs=pl.BlockSpec((1, users, other), lambda g: (g, 0, 0)),
        cost_estimate=pl.CostEstimate(flops=users * items, bytes_accessed=8 * users * items, transcendentals=0),
        name="mask_rest",
    )(block_mask, slab)


def strips_kernel(k_ref, left_ref, own_ref, far_ref, out_ref, left, right):
    depth = own_ref.shape[0]
    x = pl.program_id(1)

    @pl.when(x == 0)
    def _():
        for q in range(2):
            at = jnp.where(q == 0, k_ref[0], 1 - k_ref[0]) * depth
            high, low = split(left_ref[pl.ds(pl.multiple_of(at, depth), depth), :].T, 2)
            for i, part in enumerate((high, high, low)):
                left[q, :, depth * i:depth * (i + 1)] = part

    @pl.when(pl.program_id(0) == 0)
    def _():
        for q, ref in enumerate((own_ref, far_ref)):
            high, low = split(ref[...], 2)
            for i, part in enumerate((high, low, high)):
                right[x, q, depth * i:depth * (i + 1), :] = part

    both = jnp.dot(left[0], right[x, 0], preferred_element_type=jnp.float32) + jnp.dot(
        left[1], right[x, 1], preferred_element_type=jnp.float32
    )
    cols = out_ref.shape[-1]
    for i in range(out_ref.shape[0]):
        out_ref[i, 0] = both[:, cols * i:cols * (i + 1)]


def strips(k, bands, own, far, nz, nx):
    users, width = bands.shape
    rows, cols = width // (2 * nz), own.shape[1] // nx
    here = pl.BlockSpec((users // 2, 2 * cols), lambda z, x, k: (0, x))
    out = pl.pallas_call(
        strips_kernel,
        out_shape=jax.ShapeDtypeStruct((nx, nz, rows, cols), jnp.float32),
        grid_spec=pltpu.PrefetchScalarGridSpec(
            num_scalar_prefetch=1,
            grid=(nz, nx // 2),
            in_specs=[pl.BlockSpec((users, rows), lambda z, x, k: (0, 2 * z + k[0])), here, here],
            out_specs=pl.BlockSpec((2, 1, rows, cols), lambda z, x, k: (x, z, 0, 0)),
            scratch_shapes=[
                pltpu.VMEM((2, rows, 3 * users // 2), jnp.bfloat16),
                pltpu.VMEM((nx // 2, 2, 3 * users // 2, 2 * cols), jnp.bfloat16),
            ],
        ),
        compiler_params=pltpu.CompilerParams(vmem_limit_bytes=56 * 2**20),
        cost_estimate=pl.CostEstimate(flops=6 * users * nz * rows * nx * cols, bytes_accessed=40 * 2**20, transcendentals=0),
        name="strips",
    )(k.reshape(1).astype(jnp.int32), bands, own, far)
    return out.reshape(nx * nz * rows, cols)


def shards(slab, block_mask):
    z, k, y, x = (lax.axis_index(axis) for axis in ("z", "k", "y", "x"))
    groups = lax.axis_size("y") * lax.axis_size("k")
    ncols = lax.axis_size("z") * lax.axis_size("x")
    g = lax.axis_size("k") * y + k
    pair = ncols // groups
    total_users = slab.shape[0] * ncols * groups
    high = dict(precision=lax.Precision.HIGH, preferred_element_type=jnp.float32)
    over_users = (((0,), (0,)), ((), ()))

    scale = 2.0 ** -(total_users.bit_length() // 2)
    assert scale * scale * total_users == 1.0
    band = band_columns(slab, block_mask, ncols, scale)
    rest = other_columns(slab, block_mask, ncols, lax.axis_size("y"), scale)
    bands = lax.all_gather(band, ("k", "y"), axis=0, tiled=True)
    bands, rest = lax.optimization_barrier((bands, rest))

    upper = lax.dynamic_slice_in_dim(bands, BLK * g, BLK, 1)
    lower = lax.dynamic_slice_in_dim(bands, BLK * (ncols - 1 - g), BLK, 1)
    both = lax.dot_general(jnp.concatenate([lower, upper], axis=1), bands, over_users, **high)
    padded = jnp.concatenate([jnp.zeros((BLK, BLK * ncols), jnp.float32), both[BLK:]], axis=1)
    moved = lax.dynamic_slice_in_dim(padded, BLK * g, BLK * (ncols + 1), 1)
    long = jnp.concatenate([both[:BLK], jnp.zeros((BLK, BLK), jnp.float32)], axis=1)
    lane = lax.broadcasted_iota(jnp.int32, moved.shape, 1)
    packed = jnp.where(lane < BLK * (ncols - g), long, moved)
    pieces = lax.all_to_all(packed, ("z", "x"), split_axis=0, concat_axis=0, tiled=True)
    mine = jnp.sum(pieces.reshape(ncols, BLK // ncols, -1), axis=0)
    mine, rest = lax.optimization_barrier((mine, rest))
    panel = lax.all_gather(mine, ("y", "k", "z", "x"), axis=0, tiled=True)

    own = lax.all_to_all(rest, "y", split_axis=0, concat_axis=0, tiled=True)
    own = own.reshape(-1, own.shape[-1])
    far = lax.ppermute(own, "k", [(0, 1), (1, 0)])
    partial = strips(k, bands, own, far, lax.axis_size("z"), lax.axis_size("x"))
    items = lax.psum_scatter(partial, ("x", "z"), scatter_dimension=0, tiled=True)

    place = jnp.stack([lax.axis_size("k") * z + k, lax.axis_size("x") * y + x]).astype(jnp.int32)
    block, piece = chol_piece(panel, place, BLK * ncols, BLK * pair)
    items, block, piece = lax.optimization_barrier((items, block, piece))
    return (jnp.concatenate([block, items], axis=1), piece)


def solution(mesh):
    rows, cols = mesh.devices.shape
    axes = ("z", "k", "y", "x")
    fine = Mesh(mesh.devices.reshape(rows // 2, 2, cols // 4, 4), axes)
    return jax.shard_map(
        shards,
        mesh=fine,
        in_specs=(P(axes, None), P(axes, None)),
        out_specs=(P(("z", "k"), ("y", "x")), P(("z", "k"), ("y", "x"))),
        check_vma=False,
    )
```
